32 devices in a mesh: boxes: 8 (over y, x, core), grp: 4 (over z).
Axes of the slice: x: 2, y: 2, z: 4, core: 2. Of those that a mesh axis runs over, the one named last changes fastest.
Arguments:
- sources: float32 [22, 256, 1024], P(None, 'boxes', 'grp'), may hold values from -24 to 24
- absorption: float32 [256, 1024], P('boxes', 'grp'), may hold values from 0.5 to 5
- conductance: float32 [256, 1024], P('boxes', 'grp'), may hold values from 0.1 to 1
- diffusivity: float32 [22], replicated, may hold values from 0.3 to 3
- run_lengths: int32 [8], replicated, may hold values from 1 to 3, as said below
Outputs:
- correction: float32 [22, 384, 1024], P(None, 'boxes', 'grp')
The draws below stay inside these ranges and needn't reach their ends.
Inputs may be any that keep to these rules, and one draw needn't show every extreme that they name: `run_lengths`: the lengths add up to 16, and first[b] lies between b * 2 and b * 2 + 1 for every b.
All inputs are finite; a program needn't handle non-finite values.
Results may differ from the reference program's by a relative error of at most 0.00002.
Values sent between devices are 32-bit elements; how exact they have to be, the bound alone decides.
No kernel may reach another device: no remote copies, remote signals or barrier semaphores. Data moves between devices by JAX's collectives and lax.ppermute only.
A program may use at most 64 MiB of HBM per device.

```python
import math
import jax
import jax.numpy as jnp
from jax import lax

COMP = 22
BOX_X = 16
PLANE_Y = 16
PLANE_Z = 16
OLD_DEV = 2
MOST = 3
SWEEPS = 4
NX = 256
NY = 64
N_BOXES = 8
N_GRP = 4


def draw_run_lengths(key, part):
    key = jax.random.fold_in(key, 7)
    key_drift, key_pick = jax.random.split(key)
    drift = jax.random.randint(key_drift, (N_BOXES + 1,), 0, OLD_DEV).astype(jnp.int32)
    places = lax.broadcasted_iota(jnp.int32, (N_BOXES + 1,), 0)
    drift = jnp.where((places == 0) | (places == N_BOXES), 0, drift)
    chosen = jax.random.randint(key_pick, (), 0, N_BOXES - 1).astype(jnp.int32)
    drift = jnp.where(places == chosen, 0, drift)
    drift = jnp.where(places == chosen + 1, OLD_DEV - 1, drift)
    drift = jnp.where(places == chosen + 2, 0, drift)
    return (OLD_DEV + drift[1:] - drift[:-1]).astype(jnp.int32)


def steps_of(rng, shape, pieces, smallest, top_value):
    gain = 1.0
    for axis_at, parts in pieces:
        heights = jax.random.uniform(jax.random.fold_in(jax.random.fold_in(rng, 6), axis_at), (parts,), jnp.float32, smallest / len(pieces), top_value / len(pieces))
        gain = gain * jnp.repeat(jnp.exp(heights), shape[axis_at] // parts).reshape((-1,) + (1,) * (len(shape) - 1 - axis_at))
    return gain


def normal_values(own_key, dims, spread, limit, cuts=(), kind=jnp.bfloat16):
    result = spread * jax.random.normal(own_key, dims, jnp.float32)
    if cuts:
        result = result * steps_of(own_key, dims, cuts, -0.22, 0.18)
    return jnp.clip(result, -limit, limit).astype(kind)


def setup_inputs(seed: int = 0) -> dict:
    streams_of = jax.random.split(jax.random.key(seed), 6)
    sources = normal_values(streams_of[0], (COMP, NX, NY * PLANE_Z), 4.0, 24.0, ((1, 8), (2, 4)), jnp.float32)
    absorption = jnp.clip(jnp.exp(math.log(5.0) - 2.3025851 * jax.random.uniform(streams_of[1], (NX, NY * PLANE_Z), jnp.float32) ** steps_of(streams_of[1], (NX, NY * PLANE_Z), ((0, 8), (1, 4)), -0.2, 0.2)), 0.5, 5.0)
    conductance = jnp.clip(jnp.exp(math.log(1.0) - 2.3025851 * jax.random.uniform(streams_of[2], (NX, NY * PLANE_Z), jnp.float32) ** steps_of(streams_of[2], (NX, NY * PLANE_Z), ((0, 8), (1, 4)), -0.2, 0.2)), 0.1, 1.0)
    diffusivity = jnp.clip(jnp.exp(jax.random.uniform(streams_of[3], (COMP,), jnp.float32, math.log(0.3), math.log(3.0))), 0.3, 3.0)
    run_lengths = draw_run_lengths(jax.random.fold_in(streams_of[5], 71), 0)
    return {"sources": sources, "absorption": absorption, "conductance": conductance, "diffusivity": diffusivity, "run_lengths": run_lengths}


def checker(x_cells, y_cells, z_cells):
    x_index = lax.broadcasted_iota(jnp.int32, (x_cells, y_cells, z_cells), 0)
    y_index = lax.broadcasted_iota(jnp.int32, (x_cells, y_cells, z_cells), 1)
    z_index = lax.broadcasted_iota(jnp.int32, (x_cells, y_cells, z_cells), 2)
    return (x_index + y_index + z_index) % 2


def relax(solution, source, absorb, conduct, factor, neighbours, chosen):
    weights = jnp.zeros_like(conduct)
    inflow = jnp.zeros_like(source)
    for beside in neighbours:
        facing = 0.5 * (conduct + beside[-1])
        weights = weights + facing
        inflow = inflow + facing * beside[:-1]
    update = (source + factor * inflow) / (absorb + factor * weights)
    return jnp.where(chosen, update, solution)


def reference(sources, absorption, conductance, diffusivity, run_lengths):
    channels = sources.shape[0]
    x_cells = sources.shape[1]
    y_cells = PLANE_Y * N_GRP
    source = sources.reshape(channels, x_cells, y_cells, PLANE_Z)
    absorb = absorption.reshape(x_cells, y_cells, PLANE_Z)
    conduct = conductance.reshape(x_cells, y_cells, PLANE_Z)
    factor = diffusivity.reshape(channels, 1, 1, 1)
    parity = checker(x_cells, y_cells, PLANE_Z)
    solution = jnp.zeros_like(source)
    for half_sweep in range(SWEEPS):
        stacked = jnp.concatenate([solution, conduct[None]], 0)
        padded = jnp.pad(stacked, ((0, 0), (1, 1), (1, 1), (0, 0)))
        neighbours = [padded[:, :-2, 1:-1], padded[:, 2:, 1:-1], padded[:, 1:-1, :-2], padded[:, 1:-1, 2:], jnp.roll(stacked, 1, 3), jnp.roll(stacked, -1, 3)]
        solution = relax(solution, source, absorb, conduct, factor, neighbours, parity == half_sweep % 2)
    row_count = MOST * BOX_X
    lengths = run_lengths.astype(jnp.int32)
    firsts = (jnp.cumsum(lengths) - lengths).astype(jnp.int32)
    row_index = lax.broadcasted_iota(jnp.int32, (N_BOXES, row_count), 1)
    target = firsts[:, None] * BOX_X + row_index
    active = row_index < lengths[:, None] * BOX_X
    pick_rows = jnp.where(active, target, 0).reshape(-1).astype(jnp.int32)
    flattened = solution.reshape(channels, x_cells, y_cells * PLANE_Z)
    chosen_rows = jnp.take(flattened, pick_rows, axis=1)
    return jnp.where(active.reshape(1, -1, 1), chosen_rows, jnp.zeros_like(chosen_rows))
```

```python
import jax
import jax.numpy as jnp
from jax import lax
from jax.experimental import pallas as pl
from jax.experimental.pallas import tpu as pltpu
from jax.sharding import PartitionSpec as P

BOX_X = 16
PLANE_Z = 16
OLD_DEV = 2
MOST = 3
LANES = 128
PAIRS = 32
RIM = 64
VMEM_LIMIT = 48 * 1024 * 1024


def swap_pairs(count, first):
    lower = range(first, count - 1, 2)
    return [(i, i + 1) for i in lower] + [(i + 1, i) for i in lower]


def lane_places(rows):
    lane = lax.broadcasted_iota(jnp.int32, (rows, LANES), 1)
    even = (lane + lane // PLANE_Z) % 2 == 0
    return lane, even


def fold(ref, layer, tile, even):
    low = ref[tile, layer, pl.ds(0, 16, stride=2)]
    high = ref[tile, layer, pl.ds(1, 16, stride=2)]
    return jnp.where(even, low, high), jnp.where(even, high, low)


def pack_rims(
    src_ref, absorb_ref, conduct_ref, own_ref, first_ref, second_ref, box_ref, tiles_ref, sems
):
    channels = src_ref.shape[0]
    copies = []
    for tile in range(2):
        lanes = pl.ds(tile * LANES, LANES)
        for i, (source, place) in enumerate(
            [
                (src_ref.at[:, :, lanes], tiles_ref.at[tile, 0:channels]),
                (absorb_ref.at[:, lanes], tiles_ref.at[tile, channels]),
                (conduct_ref.at[:, lanes], tiles_ref.at[tile, channels + 1]),
            ]
        ):
            copies.append(pltpu.make_async_copy(source, place, sems.at[tile, i]))
    for copy in copies:
        copy.start()
    for copy in copies:
        copy.wait()
    lane, even = lane_places(16)
    low_half = lane < RIM
    even_group = lax.axis_index("grp") % 2 == 0

    def step(place, carry):
        red, black = zip(*[fold(tiles_ref, place, tile, even) for tile in range(2)])
        for tile in range(2):
            lanes = pl.ds(tile * LANES, LANES)
            own_ref[place, 0:16, lanes] = red[tile]
            own_ref[place, 16:32, lanes] = black[tile]
            box_ref[place, 0:8, lanes] = red[tile][:8]
            box_ref[place, 8:16, lanes] = black[tile][:8]
        low_rim = jnp.where(low_half, red[0], pltpu.roll(black[0], RIM, 1))
        high_rim = jnp.where(low_half, pltpu.roll(red[1], RIM, 1), black[1])
        first_ref[place] = jnp.where(even_group, high_rim, low_rim)
        second_ref[place] = jnp.where(even_group, low_rim, high_rim)
        return carry

    lax.fori_loop(0, channels + 2, step, 0)


def halo_tile(first_ref, second_ref, layer, low_half, even_group):
    first, second = first_ref[layer], second_ref[layer]
    above = jnp.where(even_group, first, second)
    below = jnp.where(even_group, second, first)
    red = jnp.where(low_half, above, pltpu.roll(below, RIM, 1))
    black = jnp.where(low_half, pltpu.roll(above, RIM, 1), below)
    return red, black


def pack_faces(own_ref, first_ref, second_ref, chip_ref, far_ref):
    layers = own_ref.shape[0]
    lane, _ = lane_places(16)
    low_half = lane < RIM
    even_group = lax.axis_index("grp") % 2 == 0
    even_box = lax.axis_index("boxes") % 2 == 0

    def layer_of(layer, conduct=False):
        halo_red, halo_black = halo_tile(first_ref, second_ref, layer, low_half, even_group)
        chip_ref[layer, 0:8] = halo_red[:8]
        far_ref[layer, 0:8] = halo_red[:8]
        chip_ref[layer, 8:16] = halo_black[:8]
        far_ref[layer, 8:16] = halo_black[:8]

        def rows(near, next_one):
            def row(colour, pair, tile):
                if tile < 2:
                    return own_ref[layer, pl.ds(16 * colour + pair, 1), pl.ds(tile * LANES, LANES)]
                return (halo_red, halo_black)[colour][pair : pair + 1]

            kept = [(0, near, 0), (0, near, 1), (0, near, 2), (0, next_one, 0), (0, next_one, 1)]
            kept += [(1, near, 0), (1, near, 1), (1, near, 2)]
            extra = [(0, next_one, 2), (1, next_one, 0), (1, next_one, 1), (1, next_one, 2)]
            return [row(*place) for place in kept], [row(*place) for place in extra]

        down, down_extra = rows(8, 9)
        up, up_extra = rows(15, 14)
        for i, (to_before, to_after) in enumerate(zip(down, up)):
            chip_ref[layer, 16 + i : 17 + i] = jnp.where(even_box, to_after, to_before)
            far_ref[layer, 16 + i : 17 + i] = jnp.where(even_box, to_before, to_after)
        if conduct:
            chip_ref[layers, 4:24] = jnp.zeros((20, LANES), jnp.float32)
            far_ref[layers, 4:24] = jnp.zeros((20, LANES), jnp.float32)
            for i, (to_before, to_after) in enumerate(zip(down_extra, up_extra)):
                chip_ref[layers, i : i + 1] = jnp.where(even_box, to_after, to_before)
                far_ref[layers, i : i + 1] = jnp.where(even_box, to_before, to_after)

    def step(layer, carry):
        layer_of(layer)
        return carry

    lax.fori_loop(0, layers - 1, step, 0)
    layer_of(layers - 1, True)


def z_up(x, z):
    return jnp.where(z == PLANE_Z - 1, pltpu.roll(x, PLANE_Z - 1, 1), pltpu.roll(x, LANES - 1, 1))


def z_down(x, z):
    return jnp.where(z == 0, pltpu.roll(x, LANES - PLANE_Z + 1, 1), pltpu.roll(x, 1, 1))


def around(tiles, lane, even, red, wanted=(0, 1, 2)):
    z = lane % PLANE_Z
    up = [pltpu.roll(x, LANES - PLANE_Z, 1) for x in tiles]
    down = [pltpu.roll(x, PLANE_Z, 1) for x in tiles]
    result = []
    for j in wanted:
        x = tiles[j]
        after = pltpu.roll(x, PAIRS - 1, 0)
        before = pltpu.roll(x, 1, 0)
        result.append(
            [
                x,
                jnp.where(even, before, after) if red else jnp.where(even, after, before),
                z_up(x, z),
                z_down(x, z),
                jnp.where(lane < LANES - PLANE_Z, up[j], up[(j + 1) % 3]),
                jnp.where(lane < PLANE_Z, down[(j + 2) % 3], down[j]),
            ]
        )
    return result


def smooth(
    lengths_ref, factor_ref, own_ref, first_ref, second_ref, box_ref, chip_ref, far_ref, out_ref,
    weight_ref, red_face, black_face, red_ref, black_ref, placed_ref, sems,
):
    layers = own_ref.shape[0]
    channels = layers - 2
    position = lax.axis_index("boxes")
    group = lax.axis_index("grp")
    even_box = position % 2 == 0
    even_group = group % 2 == 0
    last_box = position == lax.axis_size("boxes") - 1
    lane, even = lane_places(PAIRS)
    low_half = lane[:16] < RIM
    sub = lax.broadcasted_iota(jnp.int32, (8, LANES), 0)

    def assemble(layer, conduct=False):
        halo = halo_tile(first_ref, second_ref, layer, low_half, even_group)
        chip, far = chip_ref[layer], far_ref[layer]
        down = jnp.where(even_box, chip, far)
        up = jnp.where(even_box, far[16:], chip[16:])
        rows = lambda x: {(0, 0, 0): x[0:1], (0, 0, 1): x[1:2], (0, 0, 2): x[2:3], (0, 1, 0): x[3:4],
                          (0, 1, 1): x[4:5], (1, 0, 0): x[5:6], (1, 0, 1): x[6:7], (1, 0, 2): x[7:8]}
        down_rows, up_rows = rows(down[16:]), rows(up)
        if conduct:
            chip, far = chip_ref[layers, 0:8], far_ref[layers, 0:8]
            down_more = jnp.where(even_box, chip, far)
            up_more = jnp.where(even_box, far, chip)
            for i, key in enumerate([(0, 1, 2), (1, 1, 0), (1, 1, 1), (1, 1, 2)]):
                down_rows[key], up_rows[key] = down_more[i : i + 1], up_more[i : i + 1]
        colours = []
        for colour in range(2):
            tiles = []
            for j in range(3):
                if j < 2:
                    lanes = pl.ds(j * LANES, LANES)
                    own = own_ref[layer, 16 * colour : 16 * colour + 16, lanes]
                    box = box_ref[layer, 8 * colour : 8 * colour + 8, lanes]
                else:
                    own, box = halo[colour], down[8 * colour : 8 * colour + 8]
                spread = lambda x: jnp.broadcast_to(x, (8, LANES))
                edge = jnp.where(sub == 0, spread(down_rows[colour, 0, j]), 0.0)
                edge = jnp.where(sub == 7, spread(up_rows[colour, 0, j]), edge)
                if (colour, 1, j) in down_rows:
                    edge = jnp.where(sub == 1, spread(down_rows[colour, 1, j]), edge)
                    edge = jnp.where(sub == 6, spread(up_rows[colour, 1, j]), edge)
                tiles.append(jnp.concatenate([own, box, edge], 0))
            colours.append(tiles)
        return colours

    absorb = assemble(channels)
    conduct = assemble(channels + 1, True)
    for colour, face_ref in ((0, red_face), (1, black_face)):
        beside = around(conduct[1 - colour], lane, even, colour == 0)
        for j in range(3):
            total = jnp.zeros((PAIRS, LANES), jnp.float32)
            for i, other in enumerate(beside[j]):
                face = conduct[colour][j] + other
                face_ref[i, j] = face
                total = total + face
            weight_ref[colour, 0, j] = absorb[colour][j]
            weight_ref[colour, 1, j] = total

    pair = lax.broadcasted_iota(jnp.int32, (PAIRS, LANES), 0)
    no_after = jnp.where(last_box, 16, 26)
    no_before = jnp.where(position == 0, 32, 30)
    in_x = (pair < no_after) | (pair >= no_before)
    has_above = jnp.where(group == lax.axis_size("grp") - 1, 0, RIM)
    has_below = jnp.where(group == 0, LANES, RIM)
    in_y = (lane < has_above) | (lane >= has_below)
    inside = [in_x, in_x, in_x & in_y]

    box_count = lengths_ref[position]
    first_box = lax.fori_loop(0, position, lambda i, total: total + lengths_ref[i], jnp.int32(0))
    start = pl.multiple_of((first_box - position * OLD_DEV) * (BOX_X // 2), 8)

    def component(c, carry):
        source = assemble(c)
        factor = 0.5 * factor_ref[c]
        inverse = [
            [
                jnp.where(inside[j], 1.0 / (weight_ref[k, 0, j] + factor * weight_ref[k, 1, j]), 0.0)
                for j in range(3)
            ]
            for k in range(2)
        ]

        def update(colour, others, face_ref, wanted=(0, 1, 2)):
            result = []
            for j, beside in zip(wanted, around(others, lane, even, colour == 0, wanted)):
                inflow = face_ref[0, j] * beside[0]
                for i in range(1, 6):
                    inflow = inflow + face_ref[i, j] * beside[i]
                result.append((source[colour][j] + factor * inflow) * inverse[colour][j])
            return result

        red = [source[0][j] * inverse[0][j] for j in range(3)]
        black = update(1, red, black_face)
        red = update(0, black, red_face)
        black = update(1, red, black_face, (0, 1))
        for j in range(2):
            red_ref[j], black_ref[j] = red[j], black[j]
        for k in range(MOST):
            live = k < box_count
            for j in range(2):
                reds = red_ref[j, pl.ds(start + 8 * k, 8)]
                blacks = black_ref[j, pl.ds(start + 8 * k, 8)]
                low = jnp.where(live, jnp.where(even[:8], reds, blacks), 0.0)
                high = jnp.where(live, jnp.where(even[:8], blacks, reds), 0.0)
                placed_ref[j, c, pl.ds(BOX_X * k, 8, stride=2)] = low
                placed_ref[j, c, pl.ds(BOX_X * k + 1, 8, stride=2)] = high
        return carry

    copies = []
    half = channels // 2
    for part, (begin, end) in enumerate([(0, half), (half, channels)]):
        lax.fori_loop(begin, end, component, 0)
        for j in range(2):
            copy = pltpu.make_async_copy(
                placed_ref.at[j, begin:end],
                out_ref.at[begin:end, :, pl.ds(j * LANES, LANES)],
                sems.at[part, j],
            )
            copy.start()
            copies.append(copy)
    for copy in copies:
        copy.wait()


def in_vmem(count):
    return [pl.BlockSpec(memory_space=pltpu.VMEM)] * count


def on_device(sources, absorption, conductance, diffusivity, run_lengths):
    channels, planes, cells = sources.shape
    boxes, groups = lax.axis_size("boxes"), lax.axis_size("grp")
    layers = channels + 2
    real = lambda *shape: jax.ShapeDtypeStruct(shape, jnp.float32)
    params = pltpu.CompilerParams(vmem_limit_bytes=VMEM_LIMIT)
    own, first, second, box = pl.pallas_call(
        pack_rims,
        out_shape=(real(layers, planes, cells), real(layers, 16, LANES), real(layers, 16, LANES),
                   real(layers, 16, cells)),
        in_specs=[pl.BlockSpec(memory_space=pl.ANY)] * 3,
        out_specs=tuple(in_vmem(4)),
        scratch_shapes=[
            pltpu.VMEM((2, layers, planes, LANES), jnp.float32),
            pltpu.SemaphoreType.DMA((2, 3)),
        ],
        compiler_params=params,
    )(sources, absorption, conductance)
    first = lax.ppermute(first, "grp", swap_pairs(groups, 0))
    second = lax.ppermute(second, "grp", swap_pairs(groups, 1))
    box = lax.ppermute(box, "boxes", [(i + 1, i) for i in range(boxes - 1)])
    chip, far = pl.pallas_call(
        pack_faces,
        out_shape=(real(layers + 1, 24, LANES),) * 2,
        in_specs=in_vmem(3),
        out_specs=tuple(in_vmem(2)),
        compiler_params=params,
    )(own, first, second)
    chip = lax.ppermute(chip, "boxes", swap_pairs(boxes, 0))
    far = lax.ppermute(far, "boxes", swap_pairs(boxes, 1))
    smem = pl.BlockSpec(memory_space=pltpu.SMEM)
    return pl.pallas_call(
        smooth,
        out_shape=real(channels, MOST * BOX_X, cells),
        in_specs=[smem, smem] + in_vmem(6),
        out_specs=pl.BlockSpec(memory_space=pl.ANY),
        scratch_shapes=[
            pltpu.VMEM((2, 2, 3, PAIRS, LANES), jnp.float32),
            pltpu.VMEM((6, 3, PAIRS, LANES), jnp.float32),
            pltpu.VMEM((6, 3, PAIRS, LANES), jnp.float32),
            pltpu.VMEM((2, PAIRS, LANES), jnp.float32),
            pltpu.VMEM((2, PAIRS, LANES), jnp.float32),
            pltpu.VMEM((2, channels, MOST * BOX_X, LANES), jnp.float32),
            pltpu.SemaphoreType.DMA((2, 2)),
        ],
        compiler_params=params,
    )(run_lengths, diffusivity, own, first, second, box, chip, far)


def solution(mesh):
    return jax.shard_map(
        on_device,
        mesh=mesh,
        in_specs=(P(None, "boxes", "grp"), P("boxes", "grp"), P("boxes", "grp"), P(), P()),
        out_specs=P(None, "boxes", "grp"),
        check_vma=False,
    )
```

```python
import jax
import jax.numpy as jnp
from jax import lax
from jax.experimental import pallas as pl
from jax.experimental.pallas import tpu as pltpu
from jax.sharding import PartitionSpec as P

BOX_X = 16
PLANE_Z = 16
OLD_DEV = 2
MOST = 3
LANES = 128
SUBS = 8
RING = 32
RIM = 64
VMEM_LIMIT = 40 * 1024 * 1024
F32 = jnp.float32


def swap_pairs(count, first):
    lower = range(first, count - 1, 2)
    return [(i, i + 1) for i in lower] + [(i + 1, i) for i in lower]


def lane_places(rows):
    lane = lax.broadcasted_iota(jnp.int32, (rows, LANES), 1)
    even = (lane + lane // PLANE_Z) % 2 == 0
    return lane, even


def roll(x, shift):
    return pltpu.roll(x, shift % LANES, 1)


def pack_rim(red, black, lane):
    first = jnp.where(lane < 64, red[0], roll(red[1], 64))
    first = jnp.where((lane >= 48) & (lane < 64), roll(black[2], 48), first)
    first = jnp.where(lane >= 112, roll(black[2], 96), first)
    second = jnp.where(lane < 32, black[0], jnp.where(lane < 64, roll(black[1], 32), roll(red[2], 64)))
    return first, second


def unpack_rim(first, second, lane):
    black = jnp.where(lane < 16, roll(first, -48), roll(first, -96))
    return [first, roll(first, -64), roll(second, -64)], [second, roll(second, -32), black]


def pack_halo(red, black, lane):
    gap = (lane >= 48) & (lane < 80)
    wide = (lane >= 32) & (lane < 96)
    return [
        jnp.where(gap, roll(black[2], 48), red[0]),
        jnp.where(gap, roll(black[2], -48), red[1]),
        red[2],
        jnp.where(wide, roll(black[1], 64), black[0]),
    ]


def unpack_halo(parts, lane):
    black = jnp.where(lane < 64, roll(parts[0], -48), roll(parts[1], 48))
    return parts[:3], [parts[3], roll(parts[3], 64), black]


def pack_rims(
    src_ref, absorb_ref, conduct_ref,
    own_ref, plane_ref, first_ref, second_ref, box_ref,
    tiles_ref, sems,
):
    channels, planes, _ = src_ref.shape
    layers = channels + 2
    half = planes // 2
    copies = []
    for tile in range(2):
        lanes = pl.ds(tile * LANES, LANES)
        for i, (source, place, count) in enumerate(
            [
                (src_ref.at[:, :, lanes], 0, channels),
                (absorb_ref.at[:, lanes], channels, None),
                (conduct_ref.at[:, lanes], channels + 1, None),
            ]
        ):
            into = tiles_ref.at[tile, place] if count is None else tiles_ref.at[tile, pl.ds(0, count)]
            copies.append(pltpu.make_async_copy(source, into, sems.at[tile, i]))
    for copy in copies:
        copy.start()
    for copy in copies:
        copy.wait()

    lane, even = lane_places(SUBS)
    even_group = lax.axis_index("grp") % 2 == 0
    flat = tiles_ref.reshape(2 * layers * planes, LANES)

    def step(p, carry):
        reds, blacks = [], []
        for j in range(2):
            red, black = [], []
            for ct in range(3):
                row = (j * layers + ct * SUBS) * planes + 2 * p
                low = flat[pl.ds(row, SUBS, stride=planes)]
                high = flat[pl.ds(row + 1, SUBS, stride=planes)]
                red.append(jnp.where(even, low, high))
                black.append(jnp.where(even, high, low))
                own_ref[0, ct, p, j] = red[ct]
                own_ref[1, ct, p, j] = black[ct]
            reds.append(red)
            blacks.append(black)
        low_rim = pack_rim(reds[0], blacks[0], lane)
        high_rim = pack_rim([roll(x, 48) for x in reds[1]], [roll(x, 32) for x in blacks[1]], lane)
        for i in range(2):
            first_ref[2 * p + i] = jnp.where(even_group, high_rim[i], low_rim[i])
            second_ref[2 * p + i] = jnp.where(even_group, low_rim[i], high_rim[i])
        return carry

    lax.fori_loop(0, half, step, 0)

    for q in range(2):
        compact = []
        for j in range(2):
            row = (j * layers + channels + 1) * planes + 16 * q
            low = flat[pl.ds(row, SUBS, stride=2)]
            high = flat[pl.ds(row + 1, SUBS, stride=2)]
            compact.append((jnp.where(even, low, high), jnp.where(even, high, low)))
            for colour in range(2):
                plane_ref[colour, j, q] = compact[j][colour]
                if q == 0:
                    box_ref[96 + 2 * colour + j] = compact[j][colour]
        low_rim = jnp.where(lane < RIM, compact[0][0], roll(compact[0][1], RIM))
        high_rim = jnp.where(lane < RIM, roll(compact[1][0], RIM), compact[1][1])
        first_ref[2 * half + q] = jnp.where(even_group, high_rim, low_rim)
        second_ref[2 * half + q] = jnp.where(even_group, low_rim, high_rim)

    def copy_box(p, carry):
        for colour in range(2):
            for ct in range(3):
                for j in range(2):
                    box_ref[((colour * 3 + ct) * 8 + p) * 2 + j] = own_ref[colour, ct, p, j]
        return carry

    lax.fori_loop(0, 8, copy_box, 0)


def pack_faces(own_ref, plane_ref, first_ref, second_ref, rim_ref, rim_plane_ref, chip_ref, far_ref):
    pairs = own_ref.shape[2]
    lane, _ = lane_places(SUBS)
    low_half = lane < RIM
    even_group = lax.axis_index("grp") % 2 == 0
    even_box = lax.axis_index("boxes") % 2 == 0

    def sides(i):
        first, second = first_ref[i], second_ref[i]
        return jnp.where(even_group, first, second), jnp.where(even_group, second, first)

    def step(p, carry):
        above, below = zip(*[sides(2 * p + i) for i in range(2)])
        above, below = unpack_rim(*above, lane), unpack_rim(*below, lane)
        reds, blacks = [], []
        for ct in range(3):
            reds.append(jnp.where(low_half, above[0][ct], roll(below[0][ct], -48)))
            blacks.append(jnp.where(low_half, above[1][ct], roll(below[1][ct], -32)))
            rim_ref[0, ct, p] = reds[ct]
            rim_ref[1, ct, p] = blacks[ct]
        return reds, blacks

    def with_halo(p, carry):
        reds, blacks = step(p, carry)
        for i, part in enumerate(pack_halo(reds, blacks, lane)):
            chip_ref[4 * p + i] = part
            far_ref[4 * p + i] = part
        return carry

    def without_halo(p, carry):
        step(p, carry)
        return carry

    lax.fori_loop(0, 8, with_halo, 0)
    lax.fori_loop(8, pairs, without_halo, 0)
    for q in range(2):
        above, below = sides(2 * pairs + q)
        rim_plane_ref[0, q] = jnp.where(low_half, above, roll(below, RIM))
        rim_plane_ref[1, q] = jnp.where(low_half, roll(above, RIM), below)

    def put(i, to_before, to_after):
        chip_ref[i] = jnp.where(even_box, to_after, to_before)
        far_ref[i] = jnp.where(even_box, to_before, to_after)

    def piece(colour, ct, p, j):
        return own_ref[colour, ct, p, j] if j < 2 else rim_ref[colour, ct, p]

    for ct in range(3):
        for i, (colour, near, j) in enumerate(EDGE):
            down, up = (8, 15) if near else (9, 14)
            put(32 + ct * 8 + i, piece(colour, ct, down, j), piece(colour, ct, up, j))
    for colour in range(2):
        chip_ref[56 + colour] = rim_plane_ref[colour, 0]
        far_ref[56 + colour] = rim_plane_ref[colour, 0]
    for colour in range(2):
        for near in range(2):
            for j in range(3):
                down, up = (0, 7) if near else (1, 6)
                rows = [
                    (plane_ref[colour, j, 1] if j < 2 else rim_plane_ref[colour, 1])[k : k + 1]
                    for k in (down, up)
                ]
                k = colour * 6 + near * 3 + j
                chip_ref[58 + k // 8, k % 8 : k % 8 + 1] = jnp.where(even_box, rows[1], rows[0])
                far_ref[58 + k // 8, k % 8 : k % 8 + 1] = jnp.where(even_box, rows[0], rows[1])
    chip_ref[59, 4:8] = jnp.zeros((4, LANES), F32)
    far_ref[59, 4:8] = jnp.zeros((4, LANES), F32)


EDGE = [(0, 1, 0), (0, 1, 1), (0, 1, 2), (0, 0, 0), (0, 0, 1), (1, 1, 0), (1, 1, 1), (1, 1, 2)]


def z_up(x, z):
    return jnp.where(z == PLANE_Z - 1, roll(x, PLANE_Z - 1), roll(x, -1))


def z_down(x, z):
    return jnp.where(z == 0, roll(x, 1 - PLANE_Z), roll(x, 1))


def lane_neighbours(tiles, lane, wanted=(0, 1, 2)):
    z = lane % PLANE_Z
    up = [roll(x, -PLANE_Z) for x in tiles]
    down = [roll(x, PLANE_Z) for x in tiles]
    return [
        [
            z_up(tiles[j], z),
            z_down(tiles[j], z),
            jnp.where(lane < LANES - PLANE_Z, up[j], up[(j + 1) % 3]),
            jnp.where(lane < PLANE_Z, down[(j + 2) % 3], down[j]),
        ]
        for j in wanted
    ]


def smooth(
    lengths_ref, factor_ref, own_ref, plane_ref, rim_ref, rim_plane_ref, box_ref, chip_ref, far_ref,
    out_ref,
    face_ref, weight_ref, box_rim_ref, edge_ref, inverse_ref, value_ref, placed_ref, sems,
):
    channels, rows, _ = out_ref.shape
    position = lax.axis_index("boxes")
    group = lax.axis_index("grp")
    even_box = position % 2 == 0
    last_box = position == lax.axis_size("boxes") - 1
    lane, even = lane_places(SUBS)
    sub = lax.broadcasted_iota(jnp.int32, (SUBS, LANES), 0)
    tiles = range(3)

    def from_after(i):
        return jnp.where(even_box, chip_ref[i], far_ref[i])

    def from_before(i):
        return jnp.where(even_box, far_ref[i], chip_ref[i])

    edges = [[jnp.concatenate([get(58), get(59)], 0) for get in (from_after, from_before)]][0]
    conduct = []
    for colour in range(2):
        planes = []
        for j in tiles:
            own = [plane_ref[colour, j, q] if j < 2 else rim_plane_ref[colour, q] for q in range(2)]
            box = box_ref[96 + 2 * colour + j] if j < 2 else from_after(56 + colour)
            edge = jnp.zeros((SUBS, LANES), F32)
            for place, side, near in ((0, 0, 1), (1, 0, 0), (6, 1, 0), (7, 1, 1)):
                k = colour * 6 + near * 3 + j
                edge = jnp.where(sub == place, jnp.broadcast_to(edges[side][k : k + 1], sub.shape), edge)
            planes.append(jnp.concatenate(own + [box, edge], 0))
        conduct.append(planes)
    wide_lane, wide_even = lane_places(RING)
    for colour in range(2):
        others = conduct[1 - colour]
        beside = lane_neighbours(others, wide_lane)
        for j in tiles:
            after, before = pltpu.roll(others[j], RING - 1, 0), pltpu.roll(others[j], 1, 0)
            across = jnp.where(wide_even, *((before, after) if colour == 0 else (after, before)))
            total = jnp.zeros((RING, LANES), F32)
            for i, other in enumerate([others[j], across] + beside[j]):
                face = conduct[colour][j] + other
                face_ref[colour, i, j] = face
                total = total + face
            weight_ref[colour, j] = total

    def open_box(p, carry):
        reds, blacks = unpack_halo([from_after(4 * p + i) for i in range(4)], lane)
        for ct in range(3):
            box_rim_ref[0, ct, p], box_rim_ref[1, ct, p] = reds[ct], blacks[ct]
        return carry

    lax.fori_loop(0, 8, open_box, 0)
    for ct in range(3):
        for i in range(8):
            edge_ref[0, ct, i] = from_before(32 + ct * 8 + i)
            edge_ref[1, ct, i] = from_after(32 + ct * 8 + i)

    def own_source(q):
        p = q - 2
        return lambda colour, ct, j: own_ref[colour, ct, p, j] if j < 2 else rim_ref[colour, ct, p]

    def box_source(q):
        p = q - 18
        return lambda colour, ct, j: (
            box_ref[((colour * 3 + ct) * 8 + p) * 2 + j] if j < 2 else box_rim_ref[colour, ct, p]
        )

    def edge_source(q):
        near, side = (q in (1, 26)), int(q > 20)
        return lambda colour, ct, j: edge_ref[side, ct, EDGE.index((colour, int(near), j))]

    lane_limit = [
        None,
        None,
        (lane < jnp.where(group == lax.axis_size("grp") - 1, 0, RIM))
        | (lane >= jnp.where(group == 0, LANES, RIM)),
    ]
    factors = []
    for ct in range(3):
        factor = jnp.zeros((SUBS, LANES), F32)
        for i in range(min(SUBS, channels - ct * SUBS)):
            factor = jnp.where(sub == i, 0.5 * factor_ref[ct * SUBS + i], factor)
        factors.append(factor)

    def spread(ref, index, row):
        return jnp.broadcast_to(ref[index + (pl.ds(row, 1),)], (SUBS, LANES))

    def invert(q, colour, source, exists, wanted=(0, 1, 2)):
        row = (q + RING - 2) % RING
        for j in wanted:
            absorb = jnp.broadcast_to(source(colour, 2, j)[6:7], (SUBS, LANES))
            weight = spread(weight_ref, (colour, j), row)
            for ct in range(3):
                inverse = 1.0 / (absorb + factors[ct] * weight)
                keep = lane_limit[j]
                if exists is not None:
                    keep = exists if keep is None else keep & exists
                if keep is not None:
                    inverse = jnp.where(keep, inverse, 0.0)
                inverse_ref[colour, ct, q, j] = inverse

    def start_red(q, source, exists, wanted=(0, 1, 2)):
        invert(q, 0, source, exists, wanted)
        for j in wanted:
            for ct in range(3):
                value_ref[0, ct, q, j] = source(0, ct, j) * inverse_ref[0, ct, q, j]

    def update(q, colour, source, wanted=(0, 1, 2)):
        row = (q + RING - 2) % RING
        faces = [[spread(face_ref, (colour, i, j), row) for i in range(6)] for j in wanted]
        result = []
        for ct in range(3):
            others = [value_ref[1 - colour, ct, q, j] for j in tiles]
            beside = lane_neighbours(others, lane, wanted)
            results = []
            for j, face, near in zip(wanted, faces, beside):
                before, after = value_ref[1 - colour, ct, q - 1, j], value_ref[1 - colour, ct, q + 1, j]
                across = jnp.where(even, *((before, after) if colour == 0 else (after, before)))
                inflow = face[0] * others[j]
                for one, other in zip(face[1:], [across] + near):
                    inflow = inflow + one * other
                value = (source(colour, ct, j) + factors[ct] * inflow) * inverse_ref[colour, ct, q, j]
                results.append(value)
            result.append(results)
        return result

    def keep(q, colour, result):
        for ct in range(3):
            for j in tiles:
                value_ref[colour, ct, q, j] = result[ct][j]

    has_before, has_after = position > 0, jnp.logical_not(last_box)
    regions = [
        (2, 18, own_source, None),
        (18, 26, box_source, jnp.broadcast_to(has_after, (SUBS, LANES))),
    ]
    before_exists = jnp.broadcast_to(has_before, (SUBS, LANES))
    after_exists = regions[1][3]
    sides = [(1, 0, before_exists), (26, 27, after_exists)]

    for begin, end, source_of, exists in regions:
        def first_red(q, carry, source_of=source_of, exists=exists):
            start_red(q, source_of(q), exists)
            return carry

        lax.fori_loop(begin, end, first_red, 0)
    for near, far, exists in sides:
        start_red(near, edge_source(near), exists)

    for near, far, exists in sides:
        start_red(far, edge_source(far), exists, (0, 1))
        for ct in range(3):
            value_ref[0, ct, far, 2] = jnp.zeros((SUBS, LANES), F32)

    for near, far, exists in sides:
        invert(near, 1, edge_source(near), exists)
        keep(near, 1, update(near, 1, edge_source(near)))
    for begin, end, source_of, exists in regions:
        def first_black(q, carry, source_of=source_of, exists=exists):
            invert(q, 1, source_of(q), exists)
            keep(q, 1, update(q, 1, source_of(q)))
            return carry

        lax.fori_loop(begin, end, first_black, 0)

    for near, far, exists in sides:
        for ct in range(3):
            for j in tiles:
                value_ref[1, ct, far, j] = jnp.zeros((SUBS, LANES), F32)
        keep(near, 0, update(near, 0, edge_source(near)))
    for begin, end, source_of, exists in regions:
        def second_red(q, carry, source_of=source_of):
            keep(q, 0, update(q, 0, source_of(q)))
            return carry

        lax.fori_loop(begin, end, second_red, 0)

    box_count = lengths_ref[position]
    first_box = lax.fori_loop(0, position, lambda i, total: total + lengths_ref[i], jnp.int32(0))
    start = (first_box - position * OLD_DEV) * (BOX_X // 2)
    flat = placed_ref.reshape(2 * 3 * SUBS * rows, LANES)
    for begin, end, source_of, exists in regions:
        def second_black(q, carry, source_of=source_of):
            p = q - 2
            result = update(q, 1, source_of(q), (0, 1))
            for ct in range(3):
                for j in range(2):
                    red, black = value_ref[0, ct, q, j], result[ct][j]
                    row = (j * 3 + ct) * SUBS * rows + 2 * (p - start)
                    flat[pl.ds(row, SUBS, stride=rows)] = jnp.where(even, red, black)
                    flat[pl.ds(row + 1, SUBS, stride=rows)] = jnp.where(even, black, red)
            return carry

        lax.fori_loop(
            jnp.maximum(begin, start + 2),
            jnp.minimum(end, start + 2 + box_count * (BOX_X // 2)),
            second_black,
            0,
        )

    def clear_channel(c, carry):
        def clear_box(k, carry):
            for j in range(2):
                placed_ref[j, c, pl.ds(pl.multiple_of(k * BOX_X, BOX_X), BOX_X)] = jnp.zeros((BOX_X, LANES), F32)
            return carry

        return lax.fori_loop(box_count, MOST, clear_box, carry)

    lax.fori_loop(0, channels, clear_channel, 0)
    copies = []
    for j in range(2):
        copies.append(
            pltpu.make_async_copy(
                placed_ref.at[j, pl.ds(0, channels)], out_ref.at[:, :, pl.ds(j * LANES, LANES)], sems.at[j]
            )
        )
        copies[-1].start()
    for copy in copies:
        copy.wait()


def in_vmem(count):
    return [pl.BlockSpec(memory_space=pltpu.VMEM)] * count


def on_device(sources, absorption, conductance, diffusivity, run_lengths):
    channels, planes, cells = sources.shape
    boxes, groups = lax.axis_size("boxes"), lax.axis_size("grp")
    pairs = planes // 2
    real = lambda *shape: jax.ShapeDtypeStruct(shape + (SUBS, LANES), F32)
    vmem = lambda *shape: pltpu.VMEM(shape + (SUBS, LANES), F32)
    params = pltpu.CompilerParams(vmem_limit_bytes=VMEM_LIMIT)
    own, plane, first, second, box = pl.pallas_call(
        pack_rims,
        out_shape=(
            real(2, 3, pairs, 2),
            real(2, 2, 2),
            real(2 * pairs + 2),
            real(2 * pairs + 2),
            real(100),
        ),
        in_specs=[pl.BlockSpec(memory_space=pltpu.HBM)] * 3,
        out_specs=tuple(in_vmem(5)),
        scratch_shapes=[
            pltpu.VMEM((2, channels + 2, planes, LANES), F32),
            pltpu.SemaphoreType.DMA((2, 3)),
        ],
        compiler_params=params,
    )(sources, absorption, conductance)
    second = lax.ppermute(second, "grp", swap_pairs(groups, 1))
    first = lax.ppermute(first, "grp", swap_pairs(groups, 0))
    box = lax.ppermute(box, "boxes", [(i + 1, i) for i in range(boxes - 1)])
    rim, rim_plane, chip, far = pl.pallas_call(
        pack_faces,
        out_shape=(real(2, 3, pairs), real(2, 2), real(60), real(60)),
        in_specs=in_vmem(4),
        out_specs=tuple(in_vmem(4)),
        compiler_params=params,
    )(own, plane, first, second)
    chip = lax.ppermute(chip, "boxes", swap_pairs(boxes, 0))
    far = lax.ppermute(far, "boxes", swap_pairs(boxes, 1))
    smem = pl.BlockSpec(memory_space=pltpu.SMEM)
    return pl.pallas_call(
        smooth,
        out_shape=jax.ShapeDtypeStruct((channels, MOST * BOX_X, cells), F32),
        in_specs=[smem, smem] + in_vmem(7),
        out_specs=pl.BlockSpec(memory_space=pltpu.HBM),
        scratch_shapes=[
            pltpu.VMEM((2, 6, 3, RING, LANES), F32),
            pltpu.VMEM((2, 3, RING, LANES), F32),
            vmem(2, 3, 8),
            vmem(2, 3, 8),
            vmem(2, 3, 28, 3),
            vmem(2, 3, 28, 3),
            pltpu.VMEM((2, 3 * SUBS, MOST * BOX_X, LANES), F32),
            pltpu.SemaphoreType.DMA((2,)),
        ],
        compiler_params=params,
    )(run_lengths, diffusivity, own, plane, rim, rim_plane, box, chip, far)


def solution(mesh):
    return jax.shard_map(
        on_device,
        mesh=mesh,
        in_specs=(P(None, "boxes", "grp"), P("boxes", "grp"), P("boxes", "grp"), P(), P()),
        out_specs=P(None, "boxes", "grp"),
        check_vma=False,
    )
```

```python
import jax
import jax.numpy as jnp
from jax import lax
from jax.experimental import pallas as pl
from jax.experimental.pallas import tpu as pltpu
from jax.sharding import PartitionSpec as P

BOX_X = 16
PLANE_Z = 16
OLD_DEV = 2
MOST = 3
LANES = 128
SUBS = 8
RING = 32
RIM = 64
VMEM_LIMIT = 40 * 1024 * 1024
F32 = jnp.float32


def swap_pairs(count, first):
    lower = range(first, count - 1, 2)
    return [(i, i + 1) for i in lower] + [(i + 1, i) for i in lower]


def lane_places(rows):
    lane = lax.broadcasted_iota(jnp.int32, (rows, LANES), 1)
    even = (lane + lane // PLANE_Z) % 2 == 0
    return lane, even


def roll(x, shift):
    return pltpu.roll(x, shift % LANES, 1)


def pack_rim(red, black, lane):
    first = jnp.where(lane < 64, red[0], roll(red[1], 64))
    first = jnp.where((lane >= 48) & (lane < 64), roll(black[2], 48), first)
    first = jnp.where(lane >= 112, roll(black[2], 96), first)
    second = jnp.where(lane < 32, black[0], jnp.where(lane < 64, roll(black[1], 32), roll(red[2], 64)))
    return first, second


def unpack_rim(first, second, lane):
    black = jnp.where(lane < 16, roll(first, -48), roll(first, -96))
    return [first, roll(first, -64), roll(second, -64)], [second, roll(second, -32), black]


def pack_halo(red, black, lane):
    gap = (lane >= 48) & (lane < 80)
    wide = (lane >= 32) & (lane < 96)
    return [
        jnp.where(gap, roll(black[2], 48), red[0]),
        jnp.where(gap, roll(black[2], -48), red[1]),
        red[2],
        jnp.where(wide, roll(black[1], 64), black[0]),
    ]


def unpack_halo(parts, lane):
    black = jnp.where(lane < 64, roll(parts[0], -48), roll(parts[1], 48))
    return parts[:3], [parts[3], roll(parts[3], 64), black]


def pack_rims(
    src_ref, plain_ref,
    own_ref, plane_ref, first_ref, second_ref, box_ref,
    tiles_ref,
):
    channels, planes, _ = src_ref.shape
    layers = channels + 2
    half = planes // 2
    for layer in range(layers):
        for j in range(2):
            lanes = pl.ds(j * LANES, LANES)
            if layer < channels:
                tiles_ref[j, layer] = src_ref[layer, :, lanes]
            else:
                tiles_ref[j, layer] = plain_ref[layer - channels, :, lanes]

    lane, even = lane_places(SUBS)
    even_group = lax.axis_index("grp") % 2 == 0
    flat = tiles_ref.reshape(2 * layers * planes, LANES)

    for p in range(half):
        reds, blacks = [], []
        for j in range(2):
            red, black = [], []
            for ct in range(3):
                row = (j * layers + ct * SUBS) * planes + 2 * p
                low = flat[pl.ds(row, SUBS, stride=planes)]
                high = flat[pl.ds(row + 1, SUBS, stride=planes)]
                red.append(jnp.where(even, low, high))
                black.append(jnp.where(even, high, low))
                own_ref[0, ct, p, j] = red[ct]
                own_ref[1, ct, p, j] = black[ct]
                if p < 8:
                    box_ref[(ct * 8 + p) * 2 + j] = red[ct]
                    box_ref[((3 + ct) * 8 + p) * 2 + j] = black[ct]
            reds.append(red)
            blacks.append(black)
        low_rim = pack_rim(reds[0], blacks[0], lane)
        high_rim = pack_rim([roll(x, 48) for x in reds[1]], [roll(x, 32) for x in blacks[1]], lane)
        for i in range(2):
            first_ref[2 * p + i] = jnp.where(even_group, high_rim[i], low_rim[i])
            second_ref[2 * p + i] = jnp.where(even_group, low_rim[i], high_rim[i])

    for q in range(2):
        compact = []
        for j in range(2):
            row = (j * layers + channels + 1) * planes + 16 * q
            low = flat[pl.ds(row, SUBS, stride=2)]
            high = flat[pl.ds(row + 1, SUBS, stride=2)]
            compact.append((jnp.where(even, low, high), jnp.where(even, high, low)))
            for colour in range(2):
                plane_ref[colour, j, q] = compact[j][colour]
                if q == 0:
                    box_ref[96 + 2 * colour + j] = compact[j][colour]
        low_rim = jnp.where(lane < RIM, compact[0][0], roll(compact[0][1], RIM))
        high_rim = jnp.where(lane < RIM, roll(compact[1][0], RIM), compact[1][1])
        first_ref[2 * half + q] = jnp.where(even_group, high_rim, low_rim)
        second_ref[2 * half + q] = jnp.where(even_group, low_rim, high_rim)


def pack_faces(own_ref, plane_ref, first_ref, second_ref, rim_ref, rim_plane_ref, chip_ref, far_ref):
    pairs = own_ref.shape[2]
    lane, _ = lane_places(SUBS)
    low_half = lane < RIM
    even_group = lax.axis_index("grp") % 2 == 0
    even_box = lax.axis_index("boxes") % 2 == 0

    def sides(i):
        first, second = first_ref[i], second_ref[i]
        return jnp.where(even_group, first, second), jnp.where(even_group, second, first)

    for p in range(pairs):
        above, below = zip(*[sides(2 * p + i) for i in range(2)])
        above, below = unpack_rim(*above, lane), unpack_rim(*below, lane)
        reds, blacks = [], []
        for ct in range(3):
            reds.append(jnp.where(low_half, above[0][ct], roll(below[0][ct], -48)))
            blacks.append(jnp.where(low_half, above[1][ct], roll(below[1][ct], -32)))
            rim_ref[0, ct, p] = reds[ct]
            rim_ref[1, ct, p] = blacks[ct]
        if p < 8:
            for i, part in enumerate(pack_halo(reds, blacks, lane)):
                chip_ref[4 * p + i] = part
                far_ref[4 * p + i] = part
    for q in range(2):
        above, below = sides(2 * pairs + q)
        rim_plane_ref[0, q] = jnp.where(low_half, above, roll(below, RIM))
        rim_plane_ref[1, q] = jnp.where(low_half, roll(above, RIM), below)

    def put(i, to_before, to_after):
        chip_ref[i] = jnp.where(even_box, to_after, to_before)
        far_ref[i] = jnp.where(even_box, to_before, to_after)

    def piece(colour, ct, p, j):
        return own_ref[colour, ct, p, j] if j < 2 else rim_ref[colour, ct, p]

    for ct in range(3):
        for i, (colour, near, j) in enumerate(EDGE):
            down, up = (8, 15) if near else (9, 14)
            put(32 + ct * 8 + i, piece(colour, ct, down, j), piece(colour, ct, up, j))
    for colour in range(2):
        chip_ref[56 + colour] = rim_plane_ref[colour, 0]
        far_ref[56 + colour] = rim_plane_ref[colour, 0]
    for colour in range(2):
        for near in range(2):
            for j in range(3):
                down, up = (0, 7) if near else (1, 6)
                rows = [
                    (plane_ref[colour, j, 1] if j < 2 else rim_plane_ref[colour, 1])[k : k + 1]
                    for k in (down, up)
                ]
                k = colour * 6 + near * 3 + j
                chip_ref[58 + k // 8, k % 8 : k % 8 + 1] = jnp.where(even_box, rows[1], rows[0])
                far_ref[58 + k // 8, k % 8 : k % 8 + 1] = jnp.where(even_box, rows[0], rows[1])
    chip_ref[59, 4:8] = jnp.zeros((4, LANES), F32)
    far_ref[59, 4:8] = jnp.zeros((4, LANES), F32)


EDGE = [(0, 1, 0), (0, 1, 1), (0, 1, 2), (0, 0, 0), (0, 0, 1), (1, 1, 0), (1, 1, 1), (1, 1, 2)]


def shift_matrices():
    row = lax.broadcasted_iota(jnp.int32, (2 * LANES, LANES), 0) % LANES
    col = lax.broadcasted_iota(jnp.int32, (2 * LANES, LANES), 1)
    z = col % PLANE_Z
    pick = lambda source: jnp.where(row == source, 1.0, 0.0)
    along_z = [pick(col - z + (z + step) % PLANE_Z) for step in (1, PLANE_Z - 1)]
    along_y = [pick((col + step) % LANES) for step in (PLANE_Z, LANES - PLANE_Z)]
    return [jnp.concatenate(pair, 1).astype(jnp.bfloat16) for pair in (along_z, along_y)]


def z_up(x, z):
    return jnp.where(z == PLANE_Z - 1, roll(x, PLANE_Z - 1), roll(x, -1))


def z_down(x, z):
    return jnp.where(z == 0, roll(x, 1 - PLANE_Z), roll(x, 1))


def lane_neighbours(tiles, lane, wanted=(0, 1, 2)):
    z = lane % PLANE_Z
    up = [roll(x, -PLANE_Z) for x in tiles]
    down = [roll(x, PLANE_Z) for x in tiles]
    return [
        [
            z_up(tiles[j], z),
            z_down(tiles[j], z),
            jnp.where(lane < LANES - PLANE_Z, up[j], up[(j + 1) % 3]),
            jnp.where(lane < PLANE_Z, down[(j + 2) % 3], down[j]),
        ]
        for j in wanted
    ]


def smooth(
    lengths_ref, factor_ref, own_ref, plane_ref, rim_ref, rim_plane_ref, box_ref, chip_ref, far_ref,
    out_ref,
    face_ref, weight_ref, box_rim_ref, edge_ref, inverse_ref, value_ref, placed_ref, shift_ref, sems,
):
    channels, rows, _ = out_ref.shape
    position = lax.axis_index("boxes")
    group = lax.axis_index("grp")
    even_box = position % 2 == 0
    last_box = position == lax.axis_size("boxes") - 1
    lane, even = lane_places(SUBS)
    sub = lax.broadcasted_iota(jnp.int32, (SUBS, LANES), 0)
    tiles = range(3)

    def from_after(i):
        return jnp.where(even_box, chip_ref[i], far_ref[i])

    def from_before(i):
        return jnp.where(even_box, far_ref[i], chip_ref[i])

    edges = [[jnp.concatenate([get(58), get(59)], 0) for get in (from_after, from_before)]][0]
    conduct = []
    for colour in range(2):
        planes = []
        for j in tiles:
            own = [plane_ref[colour, j, q] if j < 2 else rim_plane_ref[colour, q] for q in range(2)]
            box = box_ref[96 + 2 * colour + j] if j < 2 else from_after(56 + colour)
            edge = jnp.zeros((SUBS, LANES), F32)
            for place, side, near in ((0, 0, 1), (1, 0, 0), (6, 1, 0), (7, 1, 1)):
                k = colour * 6 + near * 3 + j
                edge = jnp.where(sub == place, jnp.broadcast_to(edges[side][k : k + 1], sub.shape), edge)
            planes.append(jnp.concatenate(own + [box, edge], 0))
        conduct.append(planes)
    wide_lane, wide_even = lane_places(RING)
    for colour in range(2):
        others = conduct[1 - colour]
        beside = lane_neighbours(others, wide_lane)
        for j in tiles:
            after, before = pltpu.roll(others[j], RING - 1, 0), pltpu.roll(others[j], 1, 0)
            across = jnp.where(wide_even, *((before, after) if colour == 0 else (after, before)))
            total = jnp.zeros((RING, LANES), F32)
            for i, other in enumerate([others[j], across] + beside[j]):
                face = conduct[colour][j] + other
                face_ref[colour, i, j] = face
                total = total + face
            weight_ref[colour, j] = total

    for p in range(8):
        reds, blacks = unpack_halo([from_after(4 * p + i) for i in range(4)], lane)
        for ct in range(3):
            box_rim_ref[0, ct, p], box_rim_ref[1, ct, p] = reds[ct], blacks[ct]
    for ct in range(3):
        for i in range(8):
            edge_ref[0, ct, i] = from_before(32 + ct * 8 + i)
            edge_ref[1, ct, i] = from_after(32 + ct * 8 + i)

    def own_source(q):
        p = q - 2
        return lambda colour, ct, j: own_ref[colour, ct, p, j] if j < 2 else rim_ref[colour, ct, p]

    def box_source(q):
        p = q - 18
        return lambda colour, ct, j: (
            box_ref[((colour * 3 + ct) * 8 + p) * 2 + j] if j < 2 else box_rim_ref[colour, ct, p]
        )

    def edge_source(q):
        near, side = (q in (1, 26)), int(q > 20)
        return lambda colour, ct, j: edge_ref[side, ct, EDGE.index((colour, int(near), j))]

    lane_limit = [
        None,
        None,
        (lane < jnp.where(group == lax.axis_size("grp") - 1, 0, RIM))
        | (lane >= jnp.where(group == 0, LANES, RIM)),
    ]
    factors = []
    for ct in range(3):
        factor = jnp.zeros((SUBS, LANES), F32)
        for i in range(min(SUBS, channels - ct * SUBS)):
            factor = jnp.where(sub == i, 0.5 * factor_ref[ct * SUBS + i], factor)
        factors.append(factor)

    def spread(ref, index, row):
        return jnp.broadcast_to(ref[index + (pl.ds(row, 1),)], (SUBS, LANES))

    def invert(q, colour, source, exists, wanted=(0, 1, 2)):
        row = (q + RING - 2) % RING
        for j in wanted:
            absorb = jnp.broadcast_to(source(colour, 2, j)[6:7], (SUBS, LANES))
            weight = spread(weight_ref, (colour, j), row)
            for ct in range(3):
                inverse = 1.0 / (absorb + factors[ct] * weight)
                keep = lane_limit[j]
                if exists is not None:
                    keep = exists if keep is None else keep & exists
                if keep is not None:
                    inverse = jnp.where(keep, inverse, 0.0)
                inverse_ref[colour, ct, q, j] = inverse

    def start_red(q, source, exists, wanted=(0, 1, 2)):
        invert(q, 0, source, exists, wanted)
        for j in wanted:
            for ct in range(3):
                value_ref[0, ct, q, j] = source(0, ct, j) * inverse_ref[0, ct, q, j]

    for i, matrix in enumerate(shift_matrices()):
        shift_ref[i] = matrix

    def shifted(places, colour):
        index = [(ct, q, j) for q in places for ct in range(3) for j in tiles]
        x = jnp.concatenate([value_ref[colour, ct, q, j] for ct, q, j in index], 0)
        high = x.astype(jnp.bfloat16)
        both = jnp.concatenate([high, (x - high.astype(F32)).astype(jnp.bfloat16)], 1)
        moved = [jnp.dot(both, shift_ref[i], preferred_element_type=F32) for i in range(2)]
        result = {}
        for k, key in enumerate(index):
            rows = slice(k * SUBS, (k + 1) * SUBS)
            result[key] = [m[rows, i * LANES : (i + 1) * LANES] for m in moved for i in range(2)]
        return result

    def update(places, colour, wanted=(0, 1, 2)):
        moved = shifted(places, 1 - colour)
        for q in places:
            row = (q + RING - 2) % RING
            source = source_of(q)
            faces = [[spread(face_ref, (colour, i, j), row) for i in range(6)] for j in wanted]
            for ct in range(3):
                near = [moved[ct, q, j] for j in tiles]
                for j, face in zip(wanted, faces):
                    same = value_ref[1 - colour, ct, q, j]
                    before, after = value_ref[1 - colour, ct, q - 1, j], value_ref[1 - colour, ct, q + 1, j]
                    across = jnp.where(even, *((before, after) if colour == 0 else (after, before)))
                    up = jnp.where(lane < LANES - PLANE_Z, near[j][2], near[(j + 1) % 3][2])
                    down = jnp.where(lane < PLANE_Z, near[(j + 2) % 3][3], near[j][3])
                    inflow = face[0] * same
                    for one, other in zip(face[1:], [across, near[j][0], near[j][1], up, down]):
                        inflow = inflow + one * other
                    value = (source(colour, ct, j) + factors[ct] * inflow) * inverse_ref[colour, ct, q, j]
                    value_ref[colour, ct, q, j] = value

    after_exists = jnp.broadcast_to(jnp.logical_not(last_box), (SUBS, LANES))
    before_exists = jnp.broadcast_to(position > 0, (SUBS, LANES))

    def source_of(q):
        return own_source(q) if 2 <= q < 18 else box_source(q) if 18 <= q < 26 else edge_source(q)

    def exists(q):
        return before_exists if q < 2 else None if q < 18 else after_exists

    for q in range(28):
        start_red(q, source_of(q), exists(q), (0, 1) if q in (0, 27) else (0, 1, 2))
    zero = jnp.zeros((SUBS, LANES), F32)
    for q in (0, 27):
        for ct in range(3):
            value_ref[0, ct, q, 2] = zero
            for j in tiles:
                value_ref[1, ct, q, j] = zero

    blocks = [range(1, 11), range(11, 19), range(19, 27)]
    for places in blocks:
        for q in places:
            invert(q, 1, source_of(q), exists(q))
        update(places, 1)
    for places in blocks:
        update(places, 0)

    box_count = lengths_ref[position]
    first_box = lax.fori_loop(0, position, lambda i, total: total + lengths_ref[i], jnp.int32(0))
    start = first_box - position * OLD_DEV

    def send(k):
        rows = pl.ds(pl.multiple_of(k * BOX_X, BOX_X), BOX_X)
        return [
            pltpu.make_async_copy(
                placed_ref.at[j, pl.ds(0, channels), rows],
                out_ref.at[:, rows, pl.ds(j * LANES, LANES)],
                sems.at[k, j],
            )
            for j in range(2)
        ]

    flat = placed_ref.reshape(2 * 3 * SUBS * rows, LANES)
    for box in range(MOST):
        @pl.when((box >= start) & (box < start + box_count))
        def _():
            places = range(2 + box * 8, 10 + box * 8)
            update(places, 1, (0, 1))
            for q in places:
                for ct in range(3):
                    for j in range(2):
                        red, black = value_ref[0, ct, q, j], value_ref[1, ct, q, j]
                        row = (j * 3 + ct) * SUBS * rows + 2 * (q - 2 - 8 * start)
                        flat[pl.ds(row, SUBS, stride=rows)] = jnp.where(even, red, black)
                        flat[pl.ds(row + 1, SUBS, stride=rows)] = jnp.where(even, black, red)
            for copy in send(box - start):
                copy.start()

    for k in range(1, MOST):
        @pl.when(k >= box_count)
        def _():
            for j in range(2):
                for c in range(channels):
                    placed_ref[j, c, k * BOX_X : (k + 1) * BOX_X] = jnp.zeros((BOX_X, LANES), F32)
            for copy in send(k):
                copy.start()

    for k in range(MOST):
        for copy in send(k):
            copy.wait()


def in_vmem(count):
    return [pl.BlockSpec(memory_space=pltpu.VMEM)] * count


def on_device(sources, absorption, conductance, diffusivity, run_lengths):
    channels, planes, cells = sources.shape
    boxes, groups = lax.axis_size("boxes"), lax.axis_size("grp")
    pairs = planes // 2
    real = lambda *shape: jax.ShapeDtypeStruct(shape + (SUBS, LANES), F32)
    vmem = lambda *shape: pltpu.VMEM(shape + (SUBS, LANES), F32)
    params = pltpu.CompilerParams(vmem_limit_bytes=VMEM_LIMIT)
    own, plane, first, second, box = pl.pallas_call(
        pack_rims,
        out_shape=(
            real(2, 3, pairs, 2),
            real(2, 2, 2),
            real(2 * pairs + 2),
            real(2 * pairs + 2),
            real(100),
        ),
        in_specs=in_vmem(2),
        out_specs=tuple(in_vmem(5)),
        scratch_shapes=[pltpu.VMEM((2, channels + 2, planes, LANES), F32)],
        compiler_params=params,
    )(sources, jnp.stack([absorption, conductance]))
    second = lax.ppermute(second, "grp", swap_pairs(groups, 1))
    first = lax.ppermute(first, "grp", swap_pairs(groups, 0))
    box = lax.ppermute(box, "boxes", [(i + 1, i) for i in range(boxes - 1)])
    rim, rim_plane, chip, far = pl.pallas_call(
        pack_faces,
        out_shape=(real(2, 3, pairs), real(2, 2), real(60), real(60)),
        in_specs=in_vmem(4),
        out_specs=tuple(in_vmem(4)),
        compiler_params=params,
    )(own, plane, first, second)
    chip = lax.ppermute(chip, "boxes", swap_pairs(boxes, 0))
    far = lax.ppermute(far, "boxes", swap_pairs(boxes, 1))
    smem = pl.BlockSpec(memory_space=pltpu.SMEM)
    return pl.pallas_call(
        smooth,
        out_shape=jax.ShapeDtypeStruct((channels, MOST * BOX_X, cells), F32),
        in_specs=[smem, smem] + in_vmem(7),
        out_specs=pl.BlockSpec(memory_space=pltpu.HBM),
        scratch_shapes=[
            pltpu.VMEM((2, 6, 3, RING, LANES), F32),
            pltpu.VMEM((2, 3, RING, LANES), F32),
            vmem(2, 3, 8),
            vmem(2, 3, 8),
            vmem(2, 3, 28, 3),
            vmem(2, 3, 28, 3),
            pltpu.VMEM((2, 3 * SUBS, MOST * BOX_X, LANES), F32),
            pltpu.VMEM((2, 2 * LANES, 2 * LANES), jnp.bfloat16),
            pltpu.SemaphoreType.DMA((MOST, 2)),
        ],
        compiler_params=params,
    )(run_lengths, diffusivity, own, plane, rim, rim_plane, box, chip, far)


def solution(mesh):
    return jax.shard_map(
        on_device,
        mesh=mesh,
        in_specs=(P(None, "boxes", "grp"), P("boxes", "grp"), P("boxes", "grp"), P(), P()),
        out_specs=P(None, "boxes", "grp"),
        check_vma=False,
    )
```

```python
import jax
import jax.numpy as jnp
from jax import lax
from jax.experimental import pallas as pl
from jax.experimental.pallas import tpu as pltpu
from jax.sharding import PartitionSpec as P

BOX_X = 16
PLANE_Z = 16
OLD_DEV = 2
MOST = 3
LANES = 128
SUBS = 8
RING = 32
RIM = 64
VMEM_LIMIT = 40 * 1024 * 1024
F32 = jnp.float32


def swap_pairs(count, first):
    lower = range(first, count - 1, 2)
    return [(i, i + 1) for i in lower] + [(i + 1, i) for i in lower]


def lane_places(rows):
    lane = lax.broadcasted_iota(jnp.int32, (rows, LANES), 1)
    even = (lane + lane // PLANE_Z) % 2 == 0
    return lane, even


def roll(x, shift):
    return pltpu.roll(x, shift % LANES, 1)


def pack_rim(red, black, lane):
    first = jnp.where(lane < 64, red[0], roll(red[1], 64))
    first = jnp.where((lane >= 48) & (lane < 64), roll(black[2], 48), first)
    first = jnp.where(lane >= 112, roll(black[2], 96), first)
    second = jnp.where(lane < 32, black[0], jnp.where(lane < 64, roll(black[1], 32), roll(red[2], 64)))
    return first, second


def unpack_rim(first, second, lane):
    black = jnp.where(lane < 16, roll(first, -48), roll(first, -96))
    return [first, roll(first, -64), roll(second, -64)], [second, roll(second, -32), black]


def pack_halo(red, black, lane):
    gap = (lane >= 48) & (lane < 80)
    wide = (lane >= 32) & (lane < 96)
    return [
        jnp.where(gap, roll(black[2], 48), red[0]),
        jnp.where(gap, roll(black[2], -48), red[1]),
        red[2],
        jnp.where(wide, roll(black[1], 64), black[0]),
    ]


def unpack_halo(parts, lane):
    black = jnp.where(lane < 64, roll(parts[0], -48), roll(parts[1], 48))
    return parts[:3], [parts[3], roll(parts[3], 64), black]


def pack_rims(
    src_ref,
    own_ref, plane_ref, first_ref, second_ref, box_ref,
    tiles_ref,
):
    layers, planes, _ = src_ref.shape
    channels = layers - 2
    half = planes // 2
    for layer in range(layers):
        for j in range(2):
            lanes = pl.ds(j * LANES, LANES)
            tiles_ref[j, layer] = src_ref[layer, :, lanes]

    lane, even = lane_places(SUBS)
    even_group = lax.axis_index("grp") % 2 == 0
    flat = tiles_ref.reshape(2 * layers * planes, LANES)

    for p in range(half):
        reds, blacks = [], []
        for j in range(2):
            red, black = [], []
            for ct in range(3):
                row = (j * layers + ct * SUBS) * planes + 2 * p
                low = flat[pl.ds(row, SUBS, stride=planes)]
                high = flat[pl.ds(row + 1, SUBS, stride=planes)]
                red.append(jnp.where(even, low, high))
                black.append(jnp.where(even, high, low))
                own_ref[0, ct, p, j] = red[ct]
                own_ref[1, ct, p, j] = black[ct]
                if p < 8:
                    box_ref[(ct * 8 + p) * 2 + j] = red[ct]
                    box_ref[((3 + ct) * 8 + p) * 2 + j] = black[ct]
            reds.append(red)
            blacks.append(black)
        low_rim = pack_rim(reds[0], blacks[0], lane)
        high_rim = pack_rim([roll(x, 48) for x in reds[1]], [roll(x, 32) for x in blacks[1]], lane)
        for i in range(2):
            first_ref[2 * p + i] = jnp.where(even_group, high_rim[i], low_rim[i])
            second_ref[2 * p + i] = jnp.where(even_group, low_rim[i], high_rim[i])

    for q in range(2):
        compact = []
        for j in range(2):
            row = (j * layers + channels + 1) * planes + 16 * q
            low = flat[pl.ds(row, SUBS, stride=2)]
            high = flat[pl.ds(row + 1, SUBS, stride=2)]
            compact.append((jnp.where(even, low, high), jnp.where(even, high, low)))
            for colour in range(2):
                plane_ref[colour, j, q] = compact[j][colour]
        low_rim = jnp.where(lane < RIM, compact[0][0], roll(compact[0][1], RIM))
        high_rim = jnp.where(lane < RIM, roll(compact[1][0], RIM), compact[1][1])
        first_ref[2 * half + q] = jnp.where(even_group, high_rim, low_rim)
        second_ref[2 * half + q] = jnp.where(even_group, low_rim, high_rim)


def pack_faces(own_ref, plane_ref, second_ref, first_ref, rim_ref, rim_plane_ref, chip_ref, far_ref):
    pairs = own_ref.shape[2]
    lane, _ = lane_places(SUBS)
    low_half = lane < RIM
    even_group = lax.axis_index("grp") % 2 == 0
    even_box = lax.axis_index("boxes") % 2 == 0

    def sides(i):
        first, second = first_ref[i], second_ref[i]
        return jnp.where(even_group, first, second), jnp.where(even_group, second, first)

    for p in range(pairs):
        above, below = zip(*[sides(2 * p + i) for i in range(2)])
        above, below = unpack_rim(*above, lane), unpack_rim(*below, lane)
        reds, blacks = [], []
        for ct in range(3):
            reds.append(jnp.where(low_half, above[0][ct], roll(below[0][ct], -48)))
            blacks.append(jnp.where(low_half, above[1][ct], roll(below[1][ct], -32)))
            rim_ref[0, ct, p] = reds[ct]
            rim_ref[1, ct, p] = blacks[ct]
        if p < 8:
            for i, part in enumerate(pack_halo(reds, blacks, lane)):
                chip_ref[4 * p + i] = part
                far_ref[4 * p + i] = part
    for q in range(2):
        above, below = sides(2 * pairs + q)
        rim_plane_ref[0, q] = jnp.where(low_half, above, roll(below, RIM))
        rim_plane_ref[1, q] = jnp.where(low_half, roll(above, RIM), below)

    def put(i, to_before, to_after):
        chip_ref[i] = jnp.where(even_box, to_after, to_before)
        far_ref[i] = jnp.where(even_box, to_before, to_after)

    def piece(colour, ct, p, j):
        return own_ref[colour, ct, p, j] if j < 2 else rim_ref[colour, ct, p]

    for ct in range(3):
        for i, (colour, near, j) in enumerate(EDGE):
            down, up = (8, 15) if near else (9, 14)
            put(32 + ct * 8 + i, piece(colour, ct, down, j), piece(colour, ct, up, j))
    for colour in range(2):
        chip_ref[56 + colour] = rim_plane_ref[colour, 0]
        far_ref[56 + colour] = rim_plane_ref[colour, 0]
    for colour in range(2):
        for near in range(2):
            for j in range(3):
                down, up = (0, 7) if near else (1, 6)
                rows = [
                    (plane_ref[colour, j, 1] if j < 2 else rim_plane_ref[colour, 1])[k : k + 1]
                    for k in (down, up)
                ]
                k = colour * 6 + near * 3 + j
                chip_ref[58 + k // 8, k % 8 : k % 8 + 1] = jnp.where(even_box, rows[1], rows[0])
                far_ref[58 + k // 8, k % 8 : k % 8 + 1] = jnp.where(even_box, rows[0], rows[1])
    chip_ref[59, 4:8] = jnp.zeros((4, LANES), F32)
    far_ref[59, 4:8] = jnp.zeros((4, LANES), F32)


EDGE = [(0, 1, 0), (0, 1, 1), (0, 1, 2), (0, 0, 0), (0, 0, 1), (1, 1, 0), (1, 1, 1), (1, 1, 2)]


def shift_matrices():
    row = lax.broadcasted_iota(jnp.int32, (2 * LANES, LANES), 0) % LANES
    col = lax.broadcasted_iota(jnp.int32, (2 * LANES, LANES), 1)
    z = col % PLANE_Z
    pick = lambda source: jnp.where(row == source, 1.0, 0.0)
    along_z = [pick(col - z + (z + step) % PLANE_Z) for step in (1, PLANE_Z - 1)]
    along_y = [pick((col + step) % LANES) for step in (PLANE_Z, LANES - PLANE_Z)]
    return [jnp.concatenate(pair, 1).astype(jnp.bfloat16) for pair in (along_z, along_y)]


def z_up(x, z):
    return jnp.where(z == PLANE_Z - 1, roll(x, PLANE_Z - 1), roll(x, -1))


def z_down(x, z):
    return jnp.where(z == 0, roll(x, 1 - PLANE_Z), roll(x, 1))


def lane_neighbours(tiles, lane, wanted=(0, 1, 2)):
    z = lane % PLANE_Z
    up = [roll(x, -PLANE_Z) for x in tiles]
    down = [roll(x, PLANE_Z) for x in tiles]
    return [
        [
            z_up(tiles[j], z),
            z_down(tiles[j], z),
            jnp.where(lane < LANES - PLANE_Z, up[j], up[(j + 1) % 3]),
            jnp.where(lane < PLANE_Z, down[(j + 2) % 3], down[j]),
        ]
        for j in wanted
    ]


def smooth(
    lengths_ref, factor_ref, own_ref, plane_ref, rim_ref, rim_plane_ref, box_ref, far_ref, chip_ref,
    out_ref,
    face_ref, weight_ref, box_rim_ref, edge_ref, inverse_ref, value_ref, placed_ref, shift_ref, sems,
):
    channels, rows, _ = out_ref.shape
    position = lax.axis_index("boxes")
    group = lax.axis_index("grp")
    even_box = position % 2 == 0
    last_box = position == lax.axis_size("boxes") - 1
    lane, even = lane_places(SUBS)
    sub = lax.broadcasted_iota(jnp.int32, (SUBS, LANES), 0)
    tiles = range(3)

    def from_after(i):
        return jnp.where(even_box, chip_ref[i], far_ref[i])

    def from_before(i):
        return jnp.where(even_box, far_ref[i], chip_ref[i])

    edges = [[jnp.concatenate([get(58), get(59)], 0) for get in (from_after, from_before)]][0]
    flat_box = box_ref.reshape(96 * SUBS, LANES)
    conduct = []
    for colour in range(2):
        planes = []
        for j in tiles:
            own = [plane_ref[colour, j, q] if j < 2 else rim_plane_ref[colour, q] for q in range(2)]
            box = flat_box[pl.ds((((3 * colour + 2) * 8) * 2 + j) * SUBS + 7, SUBS, stride=2 * SUBS)] if j < 2 else from_after(56 + colour)
            edge = jnp.zeros((SUBS, LANES), F32)
            for place, side, near in ((0, 0, 1), (1, 0, 0), (6, 1, 0), (7, 1, 1)):
                k = colour * 6 + near * 3 + j
                edge = jnp.where(sub == place, jnp.broadcast_to(edges[side][k : k + 1], sub.shape), edge)
            planes.append(jnp.concatenate(own + [box, edge], 0))
        conduct.append(planes)
    wide_lane, wide_even = lane_places(RING)
    for colour in range(2):
        others = conduct[1 - colour]
        beside = lane_neighbours(others, wide_lane)
        for j in tiles:
            after, before = pltpu.roll(others[j], RING - 1, 0), pltpu.roll(others[j], 1, 0)
            across = jnp.where(wide_even, *((before, after) if colour == 0 else (after, before)))
            total = jnp.zeros((RING, LANES), F32)
            for i, other in enumerate([others[j], across] + beside[j]):
                face = conduct[colour][j] + other
                face_ref[colour, i, j] = face
                total = total + face
            weight_ref[colour, j] = total

    for p in range(8):
        reds, blacks = unpack_halo([from_after(4 * p + i) for i in range(4)], lane)
        for ct in range(3):
            box_rim_ref[0, ct, p], box_rim_ref[1, ct, p] = reds[ct], blacks[ct]
    for ct in range(3):
        for i in range(8):
            edge_ref[0, ct, i] = from_before(32 + ct * 8 + i)
            edge_ref[1, ct, i] = from_after(32 + ct * 8 + i)

    def own_source(q):
        p = q - 2
        return lambda colour, ct, j: own_ref[colour, ct, p, j] if j < 2 else rim_ref[colour, ct, p]

    def box_source(q):
        p = q - 18
        return lambda colour, ct, j: (
            box_ref[((colour * 3 + ct) * 8 + p) * 2 + j] if j < 2 else box_rim_ref[colour, ct, p]
        )

    def edge_source(q):
        near, side = (q in (1, 26)), int(q > 20)
        return lambda colour, ct, j: edge_ref[side, ct, EDGE.index((colour, int(near), j))]

    lane_limit = [
        None,
        None,
        (lane < jnp.where(group == lax.axis_size("grp") - 1, 0, RIM))
        | (lane >= jnp.where(group == 0, LANES, RIM)),
    ]
    factors = []
    for ct in range(3):
        factor = jnp.zeros((SUBS, LANES), F32)
        for i in range(min(SUBS, channels - ct * SUBS)):
            factor = jnp.where(sub == i, 0.5 * factor_ref[ct * SUBS + i], factor)
        factors.append(factor)

    def spread(ref, index, row):
        return jnp.broadcast_to(ref[index + (pl.ds(row, 1),)], (SUBS, LANES))

    def invert(q, colour, source, exists, wanted=(0, 1, 2)):
        row = (q + RING - 2) % RING
        for j in wanted:
            absorb = jnp.broadcast_to(source(colour, 2, j)[6:7], (SUBS, LANES))
            weight = spread(weight_ref, (colour, j), row)
            for ct in range(3):
                inverse = 1.0 / (absorb + factors[ct] * weight)
                keep = lane_limit[j]
                if exists is not None:
                    keep = exists if keep is None else keep & exists
                if keep is not None:
                    inverse = jnp.where(keep, inverse, 0.0)
                inverse_ref[colour, ct, q, j] = inverse

    def start_red(q, source, exists, wanted=(0, 1, 2)):
        invert(q, 0, source, exists, wanted)
        for j in wanted:
            for ct in range(3):
                value_ref[0, ct, q, j] = source(0, ct, j) * inverse_ref[0, ct, q, j]

    for i, matrix in enumerate(shift_matrices()):
        shift_ref[i] = matrix

    def shifted(places, colour):
        index = [(ct, q, j) for q in places for ct in range(3) for j in tiles]
        x = jnp.concatenate([value_ref[colour, ct, q, j] for ct, q, j in index], 0)
        high = x.astype(jnp.bfloat16)
        both = jnp.concatenate([high, (x - high.astype(F32)).astype(jnp.bfloat16)], 1)
        moved = [jnp.dot(both, shift_ref[i], preferred_element_type=F32) for i in range(2)]
        result = {}
        for k, key in enumerate(index):
            rows = slice(k * SUBS, (k + 1) * SUBS)
            result[key] = [m[rows, i * LANES : (i + 1) * LANES] for m in moved for i in range(2)]
        return result

    def update(places, colour, wanted=(0, 1, 2)):
        moved = shifted(places, 1 - colour)
        for q in places:
            row = (q + RING - 2) % RING
            source = source_of(q)
            faces = [[spread(face_ref, (colour, i, j), row) for i in range(6)] for j in wanted]
            for ct in range(3):
                near = [moved[ct, q, j] for j in tiles]
                for j, face in zip(wanted, faces):
                    same = value_ref[1 - colour, ct, q, j]
                    before, after = value_ref[1 - colour, ct, q - 1, j], value_ref[1 - colour, ct, q + 1, j]
                    across = jnp.where(even, *((before, after) if colour == 0 else (after, before)))
                    up = jnp.where(lane < LANES - PLANE_Z, near[j][2], near[(j + 1) % 3][2])
                    down = jnp.where(lane < PLANE_Z, near[(j + 2) % 3][3], near[j][3])
                    inflow = face[0] * same
                    for one, other in zip(face[1:], [across, near[j][0], near[j][1], up, down]):
                        inflow = inflow + one * other
                    value = (source(colour, ct, j) + factors[ct] * inflow) * inverse_ref[colour, ct, q, j]
                    value_ref[colour, ct, q, j] = value

    after_exists = jnp.broadcast_to(jnp.logical_not(last_box), (SUBS, LANES))
    before_exists = jnp.broadcast_to(position > 0, (SUBS, LANES))

    def source_of(q):
        return own_source(q) if 2 <= q < 18 else box_source(q) if 18 <= q < 26 else edge_source(q)

    def exists(q):
        return before_exists if q < 2 else None if q < 18 else after_exists

    for q in range(28):
        start_red(q, source_of(q), exists(q), (0, 1) if q in (0, 27) else (0, 1, 2))
    zero = jnp.zeros((SUBS, LANES), F32)
    for q in (0, 27):
        for ct in range(3):
            value_ref[0, ct, q, 2] = zero
            for j in tiles:
                value_ref[1, ct, q, j] = zero

    blocks = [range(1, 11), range(11, 19), range(19, 27)]
    for places in blocks:
        for q in places:
            invert(q, 1, source_of(q), exists(q))
        update(places, 1)
    for places in blocks:
        update(places, 0)

    box_count = lengths_ref[position]
    first_box = lax.fori_loop(0, position, lambda i, total: total + lengths_ref[i], jnp.int32(0))
    start = first_box - position * OLD_DEV

    def send(k):
        rows = pl.ds(pl.multiple_of(k * BOX_X, BOX_X), BOX_X)
        return [
            pltpu.make_async_copy(
                placed_ref.at[j, pl.ds(0, channels), rows],
                out_ref.at[:, rows, pl.ds(j * LANES, LANES)],
                sems.at[k, j],
            )
            for j in range(2)
        ]

    flat = placed_ref.reshape(2 * 3 * SUBS * rows, LANES)
    for box in range(MOST):
        @pl.when((box >= start) & (box < start + box_count))
        def _():
            places = range(2 + box * 8, 10 + box * 8)
            update(places, 1, (0, 1))
            for q in places:
                for ct in range(3):
                    for j in range(2):
                        red, black = value_ref[0, ct, q, j], value_ref[1, ct, q, j]
                        row = (j * 3 + ct) * SUBS * rows + 2 * (q - 2 - 8 * start)
                        flat[pl.ds(row, SUBS, stride=rows)] = jnp.where(even, red, black)
                        flat[pl.ds(row + 1, SUBS, stride=rows)] = jnp.where(even, black, red)
            for copy in send(box - start):
                copy.start()

    for k in range(1, MOST):
        @pl.when(k >= box_count)
        def _():
            for j in range(2):
                for c in range(channels):
                    placed_ref[j, c, k * BOX_X : (k + 1) * BOX_X] = jnp.zeros((BOX_X, LANES), F32)
            for copy in send(k):
                copy.start()

    for k in range(MOST):
        for copy in send(k):
            copy.wait()


def in_vmem(count):
    return [pl.BlockSpec(memory_space=pltpu.VMEM)] * count


def on_device(sources, absorption, conductance, diffusivity, run_lengths):
    channels, planes, cells = sources.shape
    boxes, groups = lax.axis_size("boxes"), lax.axis_size("grp")
    pairs = planes // 2
    real = lambda *shape: jax.ShapeDtypeStruct(shape + (SUBS, LANES), F32)
    vmem = lambda *shape: pltpu.VMEM(shape + (SUBS, LANES), F32)
    params = pltpu.CompilerParams(vmem_limit_bytes=VMEM_LIMIT)
    own, plane, first, second, box = pl.pallas_call(
        pack_rims,
        out_shape=(
            real(2, 3, pairs, 2),
            real(2, 2, 2),
            real(2 * pairs + 2),
            real(2 * pairs + 2),
            real(96),
        ),
        in_specs=in_vmem(1),
        out_specs=tuple(in_vmem(5)),
        scratch_shapes=[pltpu.VMEM((2, channels + 2, planes, LANES), F32)],
        compiler_params=params,
    )(jnp.concatenate([sources, absorption[None], conductance[None]]))
    second = lax.ppermute(second, "grp", swap_pairs(groups, 1))
    first = lax.ppermute(first, "grp", swap_pairs(groups, 0))
    box = lax.ppermute(box, "boxes", [(i + 1, i) for i in range(boxes - 1)])
    rim, rim_plane, chip, far = pl.pallas_call(
        pack_faces,
        out_shape=(real(2, 3, pairs), real(2, 2), real(60), real(60)),
        in_specs=in_vmem(4),
        out_specs=tuple(in_vmem(4)),
        cost_estimate=pl.CostEstimate(flops=5_000_000_000, bytes_accessed=0, transcendentals=0),
        compiler_params=params,
    )(own, plane, second, first)
    chip = lax.ppermute(chip, "boxes", swap_pairs(boxes, 0))
    far = lax.ppermute(far, "boxes", swap_pairs(boxes, 1))
    smem = pl.BlockSpec(memory_space=pltpu.SMEM)
    return pl.pallas_call(
        smooth,
        out_shape=jax.ShapeDtypeStruct((channels, MOST * BOX_X, cells), F32),
        in_specs=[smem, smem] + in_vmem(7),
        out_specs=pl.BlockSpec(memory_space=pltpu.HBM),
        scratch_shapes=[
            pltpu.VMEM((2, 6, 3, RING, LANES), F32),
            pltpu.VMEM((2, 3, RING, LANES), F32),
            vmem(2, 3, 8),
            vmem(2, 3, 8),
            vmem(2, 3, 28, 3),
            vmem(2, 3, 28, 3),
            pltpu.VMEM((2, 3 * SUBS, MOST * BOX_X, LANES), F32),
            pltpu.VMEM((2, 2 * LANES, 2 * LANES), jnp.bfloat16),
            pltpu.SemaphoreType.DMA((MOST, 2)),
        ],
        compiler_params=params,
    )(run_lengths, diffusivity, own, plane, rim, rim_plane, box, far, chip)


def solution(mesh):
    return jax.shard_map(
        on_device,
        mesh=mesh,
        in_specs=(P(None, "boxes", "grp"), P("boxes", "grp"), P("boxes", "grp"), P(), P()),
        out_specs=P(None, "boxes", "grp"),
        check_vma=False,
    )
```

```python
import jax
import jax.numpy as jnp
from jax import lax
from jax.experimental import pallas as pl
from jax.experimental.pallas import tpu as pltpu
from jax.sharding import PartitionSpec as P

BOX_X = 16
PLANE_Z = 16
OLD_DEV = 2
MOST = 3
LANES = 128
SUBS = 8
RING = 32
RIM = 64
VMEM_LIMIT = 40 * 1024 * 1024
F32 = jnp.float32


def swap_pairs(count, first):
    lower = range(first, count - 1, 2)
    return [(i, i + 1) for i in lower] + [(i + 1, i) for i in lower]


def lane_places(rows):
    lane = lax.broadcasted_iota(jnp.int32, (rows, LANES), 1)
    even = (lane + lane // PLANE_Z) % 2 == 0
    return lane, even


def roll(x, shift):
    return pltpu.roll(x, shift % LANES, 1)


def pack_rim(red, black, lane):
    first = jnp.where(lane < 64, red[0], roll(red[1], 64))
    first = jnp.where((lane >= 48) & (lane < 64), roll(black[2], 48), first)
    first = jnp.where(lane >= 112, roll(black[2], 96), first)
    second = jnp.where(lane < 32, black[0], jnp.where(lane < 64, roll(black[1], 32), roll(red[2], 64)))
    return first, second


def unpack_rim(first, second, lane):
    black = jnp.where(lane < 16, roll(first, -48), roll(first, -96))
    return [first, roll(first, -64), roll(second, -64)], [second, roll(second, -32), black]


def pack_halo(red, black, lane):
    gap = (lane >= 48) & (lane < 80)
    wide = (lane >= 32) & (lane < 96)
    return [
        jnp.where(gap, roll(black[2], 48), red[0]),
        jnp.where(gap, roll(black[2], -48), red[1]),
        red[2],
        jnp.where(wide, roll(black[1], 64), black[0]),
    ]


def unpack_halo(parts, lane):
    black = jnp.where(lane < 64, roll(parts[0], -48), roll(parts[1], 48))
    return parts[:3], [parts[3], roll(parts[3], 64), black]


def pack_rims(
    src_ref,
    own_ref, plane_ref, first_ref, second_ref, box_ref,
    tiles_ref,
):
    layers, planes, _ = src_ref.shape
    channels = layers - 2
    half = planes // 2
    for layer in range(layers):
        for j in range(2):
            lanes = pl.ds(j * LANES, LANES)
            tiles_ref[j, layer] = src_ref[layer, :, lanes]

    lane, even = lane_places(SUBS)
    even_group = lax.axis_index("grp") % 2 == 0
    flat = tiles_ref.reshape(2 * layers * planes, LANES)

    for p in range(half):
        reds, blacks = [], []
        for j in range(2):
            red, black = [], []
            for ct in range(3):
                row = (j * layers + ct * SUBS) * planes + 2 * p
                low = flat[pl.ds(row, SUBS, stride=planes)]
                high = flat[pl.ds(row + 1, SUBS, stride=planes)]
                red.append(jnp.where(even, low, high))
                black.append(jnp.where(even, high, low))
                own_ref[0, ct, p, j] = red[ct]
                own_ref[1, ct, p, j] = black[ct]
                if p < 8:
                    box_ref[(ct * 8 + p) * 2 + j] = red[ct]
                    box_ref[((3 + ct) * 8 + p) * 2 + j] = black[ct]
            reds.append(red)
            blacks.append(black)
        low_rim = pack_rim(reds[0], blacks[0], lane)
        high_rim = pack_rim([roll(x, 48) for x in reds[1]], [roll(x, 32) for x in blacks[1]], lane)
        for i in range(2):
            first_ref[2 * p + i] = jnp.where(even_group, high_rim[i], low_rim[i])
            second_ref[2 * p + i] = jnp.where(even_group, low_rim[i], high_rim[i])

    for q in range(2):
        compact = []
        for j in range(2):
            row = (j * layers + channels + 1) * planes + 16 * q
            low = flat[pl.ds(row, SUBS, stride=2)]
            high = flat[pl.ds(row + 1, SUBS, stride=2)]
            compact.append((jnp.where(even, low, high), jnp.where(even, high, low)))
            for colour in range(2):
                plane_ref[colour, j, q] = compact[j][colour]
        low_rim = jnp.where(lane < RIM, compact[0][0], roll(compact[0][1], RIM))
        high_rim = jnp.where(lane < RIM, roll(compact[1][0], RIM), compact[1][1])
        first_ref[2 * half + q] = jnp.where(even_group, high_rim, low_rim)
        second_ref[2 * half + q] = jnp.where(even_group, low_rim, high_rim)


def pack_faces(own_ref, plane_ref, second_ref, first_ref, rim_ref, rim_plane_ref, chip_ref, far_ref):
    pairs = own_ref.shape[2]
    lane, _ = lane_places(SUBS)
    low_half = lane < RIM
    even_group = lax.axis_index("grp") % 2 == 0
    even_box = lax.axis_index("boxes") % 2 == 0

    def sides(i):
        first, second = first_ref[i], second_ref[i]
        return jnp.where(even_group, first, second), jnp.where(even_group, second, first)

    for p in range(pairs):
        above, below = zip(*[sides(2 * p + i) for i in range(2)])
        above, below = unpack_rim(*above, lane), unpack_rim(*below, lane)
        reds, blacks = [], []
        for ct in range(3):
            reds.append(jnp.where(low_half, above[0][ct], roll(below[0][ct], -48)))
            blacks.append(jnp.where(low_half, above[1][ct], roll(below[1][ct], -32)))
            rim_ref[0, ct, p] = reds[ct]
            rim_ref[1, ct, p] = blacks[ct]
        if p < 8:
            for i, part in enumerate(pack_halo(reds, blacks, lane)):
                chip_ref[4 * p + i] = part
                far_ref[4 * p + i] = part
    for q in range(2):
        above, below = sides(2 * pairs + q)
        rim_plane_ref[0, q] = jnp.where(low_half, above, roll(below, RIM))
        rim_plane_ref[1, q] = jnp.where(low_half, roll(above, RIM), below)

    def put(i, to_before, to_after):
        chip_ref[i] = jnp.where(even_box, to_after, to_before)
        far_ref[i] = jnp.where(even_box, to_before, to_after)

    def piece(colour, ct, p, j):
        return own_ref[colour, ct, p, j] if j < 2 else rim_ref[colour, ct, p]

    for ct in range(3):
        for i, (colour, near, j) in enumerate(EDGE):
            down, up = (8, 15) if near else (9, 14)
            put(32 + ct * 8 + i, piece(colour, ct, down, j), piece(colour, ct, up, j))
    for colour in range(2):
        chip_ref[56 + colour] = rim_plane_ref[colour, 0]
        far_ref[56 + colour] = rim_plane_ref[colour, 0]
    for colour in range(2):
        for near in range(2):
            for j in range(3):
                down, up = (0, 7) if near else (1, 6)
                rows = [
                    (plane_ref[colour, j, 1] if j < 2 else rim_plane_ref[colour, 1])[k : k + 1]
                    for k in (down, up)
                ]
                k = colour * 6 + near * 3 + j
                chip_ref[58 + k // 8, k % 8 : k % 8 + 1] = jnp.where(even_box, rows[1], rows[0])
                far_ref[58 + k // 8, k % 8 : k % 8 + 1] = jnp.where(even_box, rows[0], rows[1])
    chip_ref[59, 4:8] = jnp.zeros((4, LANES), F32)
    far_ref[59, 4:8] = jnp.zeros((4, LANES), F32)


EDGE = [(0, 1, 0), (0, 1, 1), (0, 1, 2), (0, 0, 0), (0, 0, 1), (1, 1, 0), (1, 1, 1), (1, 1, 2)]


def shift_matrices():
    row = lax.broadcasted_iota(jnp.int32, (2 * LANES, LANES), 0) % LANES
    col = lax.broadcasted_iota(jnp.int32, (2 * LANES, LANES), 1)
    z = col % PLANE_Z
    pick = lambda source: jnp.where(row == source, 1.0, 0.0)
    along_z = [pick(col - z + (z + step) % PLANE_Z) for step in (1, PLANE_Z - 1)]
    along_y = [pick((col + step) % LANES) for step in (PLANE_Z, LANES - PLANE_Z)]
    return [jnp.concatenate(pair, 1).astype(jnp.bfloat16) for pair in (along_z, along_y)]


def z_up(x, z):
    return jnp.where(z == PLANE_Z - 1, roll(x, PLANE_Z - 1), roll(x, -1))


def z_down(x, z):
    return jnp.where(z == 0, roll(x, 1 - PLANE_Z), roll(x, 1))


def lane_neighbours(tiles, lane, wanted=(0, 1, 2)):
    z = lane % PLANE_Z
    up = [roll(x, -PLANE_Z) for x in tiles]
    down = [roll(x, PLANE_Z) for x in tiles]
    return [
        [
            z_up(tiles[j], z),
            z_down(tiles[j], z),
            jnp.where(lane < LANES - PLANE_Z, up[j], up[(j + 1) % 3]),
            jnp.where(lane < PLANE_Z, down[(j + 2) % 3], down[j]),
        ]
        for j in wanted
    ]


INNER = [range(1, 15), range(1, 15), range(2, 14), range(2, 14)]


class Smoother:
    def __init__(self, factor_ref, face_ref, weight_ref, inverse_ref, shift_ref, channels, ring):
        self.face_ref, self.weight_ref, self.inverse_ref = face_ref, weight_ref, inverse_ref
        self.shift_ref, self.ring = shift_ref, ring
        self.lane, self.even = lane_places(SUBS)
        sub = lax.broadcasted_iota(jnp.int32, (SUBS, LANES), 0)
        group = lax.axis_index("grp")
        above = jnp.where(group == lax.axis_size("grp") - 1, 0, LANES)
        below = jnp.where(group == 0, LANES, 0)
        self.limit = [
            ((self.lane < jnp.minimum(above, PLANE_Z * rows)))
            | (self.lane >= jnp.maximum(below, LANES - PLANE_Z * rows))
            for rows in (3, 2)
        ]
        self.factors = []
        for ct in range(3):
            factor = jnp.zeros((SUBS, LANES), F32)
            for i in range(min(SUBS, channels - ct * SUBS)):
                factor = jnp.where(sub == i, 0.5 * factor_ref[ct * SUBS + i], factor)
            self.factors.append(factor)

    def find_faces(self, conduct):
        wide_lane, wide_even = lane_places(self.ring)
        for colour in range(2):
            others = conduct[1 - colour]
            beside = lane_neighbours(others, wide_lane)
            for j in range(3):
                after, before = pltpu.roll(others[j], self.ring - 1, 0), pltpu.roll(others[j], 1, 0)
                across = jnp.where(wide_even, *((before, after) if colour == 0 else (after, before)))
                total = jnp.zeros((self.ring, LANES), F32)
                for i, other in enumerate([others[j], across] + beside[j]):
                    face = conduct[colour][j] + other
                    self.face_ref[colour, i, j] = face
                    total = total + face
                self.weight_ref[colour, j] = total

    def spread(self, ref, index, q):
        row = (q + RING - 2) % RING
        return jnp.broadcast_to(ref[index + (pl.ds(row, 1),)], (SUBS, LANES))

    def invert(self, q, colour, source, exists, wanted=(0, 1, 2)):
        for j in wanted:
            absorb = jnp.broadcast_to(source(colour, 2, j)[6:7], (SUBS, LANES))
            weight = self.spread(self.weight_ref, (colour, j), q)
            keep = exists if j < 2 else self.limit[colour]
            if exists is not None and j == 2:
                keep = keep & exists
            for ct in range(3):
                inverse = 1.0 / (absorb + self.factors[ct] * weight)
                if keep is not None:
                    inverse = jnp.where(keep, inverse, 0.0)
                self.inverse_ref[colour, ct, q, j] = inverse

    def shifted(self, places, get):
        index = [(ct, q, j) for q in places for ct in range(3) for j in range(3)]
        x = jnp.concatenate([get(*key) for key in index], 0)
        high = x.astype(jnp.bfloat16)
        both = jnp.concatenate([high, (x - high.astype(F32)).astype(jnp.bfloat16)], 1)
        moved = [jnp.dot(both, self.shift_ref[i], preferred_element_type=F32) for i in range(2)]
        result = {}
        for k, key in enumerate(index):
            rows = slice(k * SUBS, (k + 1) * SUBS)
            result[key] = [m[rows, i * LANES : (i + 1) * LANES] for m in moved for i in range(2)]
        return result

    def update(self, places, colour, get, put, source_of, wanted=(0, 1, 2)):
        lane, even = self.lane, self.even
        moved = self.shifted(places, get)
        for q in places:
            source = source_of(q)
            faces = [
                [self.spread(self.face_ref, (colour, i, j), q) for i in range(6)] for j in wanted
            ]
            for ct in range(3):
                near = [moved[ct, q, j] for j in range(3)]
                for j, face in zip(wanted, faces):
                    before, after = get(ct, q - 1, j), get(ct, q + 1, j)
                    across = jnp.where(even, *((before, after) if colour == 0 else (after, before)))
                    up = jnp.where(lane < LANES - PLANE_Z, near[j][2], near[(j + 1) % 3][2])
                    down = jnp.where(lane < PLANE_Z, near[(j + 2) % 3][3], near[j][3])
                    inflow = face[0] * get(ct, q, j)
                    for one, other in zip(face[1:], [across, near[j][0], near[j][1], up, down]):
                        inflow = inflow + one * other
                    value = source(colour, ct, j) + self.factors[ct] * inflow
                    put(ct, q, j, value * self.inverse_ref[colour, ct, q, j])


def own_run(lengths_ref):
    position = lax.axis_index("boxes")
    first_box = lax.fori_loop(0, position, lambda i, total: total + lengths_ref[i], jnp.int32(0))
    return first_box - position * OLD_DEV, lengths_ref[position]


def placer(placed_ref, start, even):
    rows = placed_ref.shape[2]
    flat = placed_ref.reshape(2 * 3 * SUBS * rows, LANES)

    def place(ct, q, j, red, black):
        row = (j * 3 + ct) * SUBS * rows + 2 * (q - 2 - 8 * start)
        flat[pl.ds(row, SUBS, stride=rows)] = jnp.where(even, red, black)
        flat[pl.ds(row + 1, SUBS, stride=rows)] = jnp.where(even, black, red)

    return place


def smooth_inner(
    lengths_ref, factor_ref, own_ref, plane_ref, rim_ref, rim_plane_ref,
    value_ref, placed_ref, shift_ref,
    face_ref, weight_ref, inverse_ref,
):
    pairs = own_ref.shape[2]
    channels = factor_ref.shape[0]
    work = Smoother(factor_ref, face_ref, weight_ref, inverse_ref, shift_ref, channels, pairs)
    for i, matrix in enumerate(shift_matrices()):
        shift_ref[i] = matrix

    def plane(colour, j):
        return [plane_ref[colour, j, k] if j < 2 else rim_plane_ref[colour, k] for k in range(2)]

    work.find_faces(
        [[jnp.concatenate(plane(colour, j), 0) for j in range(3)] for colour in range(2)]
    )

    def source_of(q):
        p = q - 2
        return lambda colour, ct, j: own_ref[colour, ct, p, j] if j < 2 else rim_ref[colour, ct, p]

    def getter(stage):
        return lambda ct, q, j: value_ref[stage, ct, q - 2, j]

    def putter(stage):
        def put(ct, q, j, value):
            value_ref[stage, ct, q - 2, j] = value

        return put

    for p in range(pairs):
        source = source_of(p + 2)
        work.invert(p + 2, 0, source, None)
        work.invert(p + 2, 1, source, None)
        for ct in range(3):
            for j in range(3):
                value_ref[0, ct, p, j] = source(0, ct, j) * inverse_ref[0, ct, p + 2, j]
    for p in (0, pairs - 1):
        for ct in range(3):
            for j in range(3):
                value_ref[1, ct, p, j] = jnp.zeros((SUBS, LANES), F32)
    for places in (range(3, 11), range(11, 17)):
        work.update(places, 1, getter(0), putter(1), source_of)
    for places in (range(3, 11), range(11, 17)):
        work.update(places, 0, getter(1), putter(2), source_of)
    for places in (range(4, 10), range(10, 16)):
        work.update(places, 1, getter(2), putter(3), source_of, (0, 1))

    start, box_count = own_run(lengths_ref)
    place = placer(placed_ref, start, work.even)
    for box, places in enumerate((range(4, 10), range(10, 16))):
        @pl.when((box >= start) & (box < start + box_count))
        def _():
            for q in places:
                for ct in range(3):
                    for j in range(2):
                        place(ct, q, j, getter(2)(ct, q, j), getter(3)(ct, q, j))

    for k in range(1, MOST):
        @pl.when(k >= box_count)
        def _():
            for j in range(2):
                for c in range(channels):
                    placed_ref[j, c, k * BOX_X : (k + 1) * BOX_X] = jnp.zeros((BOX_X, LANES), F32)


def smooth_outer(
    lengths_ref, factor_ref, own_ref, plane_ref, rim_ref, rim_plane_ref, box_ref, far_ref, chip_ref,
    inner_ref, shift_ref, given_ref,
    out_ref, placed_ref,
    face_ref, weight_ref, inverse_ref, value_ref, box_rim_ref, edge_ref, sems,
):
    channels = out_ref.shape[0]
    position = lax.axis_index("boxes")
    even_box = position % 2 == 0
    last_box = position == lax.axis_size("boxes") - 1
    work = Smoother(factor_ref, face_ref, weight_ref, inverse_ref, shift_ref, channels, RING)
    lane = work.lane
    sub = lax.broadcasted_iota(jnp.int32, (SUBS, LANES), 0)
    start, box_count = own_run(lengths_ref)

    def send(k):
        rows = pl.ds(pl.multiple_of(k * BOX_X, BOX_X), BOX_X)
        return [
            pltpu.make_async_copy(
                placed_ref.at[j, pl.ds(0, channels), rows],
                out_ref.at[:, rows, pl.ds(j * LANES, LANES)],
                sems.at[k, j],
            )
            for j in range(2)
        ]

    for k in range(1, MOST):
        @pl.when(k >= box_count)
        def _():
            for copy in send(k):
                copy.start()

    def from_after(i):
        return jnp.where(even_box, chip_ref[i], far_ref[i])

    def from_before(i):
        return jnp.where(even_box, far_ref[i], chip_ref[i])

    edges = [jnp.concatenate([get(58), get(59)], 0) for get in (from_after, from_before)]
    flat_box = box_ref.reshape(96 * SUBS, LANES)
    conduct = []
    for colour in range(2):
        planes = []
        for j in range(3):
            own = [plane_ref[colour, j, k] if j < 2 else rim_plane_ref[colour, k] for k in range(2)]
            if j < 2:
                row = (((3 * colour + 2) * 8) * 2 + j) * SUBS + 7
                box = flat_box[pl.ds(row, SUBS, stride=2 * SUBS)]
            else:
                box = from_after(56 + colour)
            edge = jnp.zeros((SUBS, LANES), F32)
            for place_at, side, near in ((0, 0, 1), (1, 0, 0), (6, 1, 0), (7, 1, 1)):
                k = colour * 6 + near * 3 + j
                row = jnp.broadcast_to(edges[side][k : k + 1], (SUBS, LANES))
                edge = jnp.where(sub == place_at, row, edge)
            planes.append(jnp.concatenate(own + [box, edge], 0))
        conduct.append(planes)
    work.find_faces(conduct)

    for p in range(8):
        reds, blacks = unpack_halo([from_after(4 * p + i) for i in range(4)], lane)
        for ct in range(3):
            box_rim_ref[0, ct, p], box_rim_ref[1, ct, p] = reds[ct], blacks[ct]
    for ct in range(3):
        for i in range(8):
            edge_ref[0, ct, i] = from_before(32 + ct * 8 + i)
            edge_ref[1, ct, i] = from_after(32 + ct * 8 + i)

    def source_of(q):
        if 2 <= q < 18:
            return lambda colour, ct, j: (
                own_ref[colour, ct, q - 2, j] if j < 2 else rim_ref[colour, ct, q - 2]
            )
        if 18 <= q < 26:
            return lambda colour, ct, j: (
                box_ref[((colour * 3 + ct) * 8 + q - 18) * 2 + j]
                if j < 2
                else box_rim_ref[colour, ct, q - 18]
            )
        near, side = int(q in (1, 26)), int(q > 20)
        return lambda colour, ct, j: edge_ref[side, ct, EDGE.index((colour, near, j))]

    after_exists = jnp.broadcast_to(jnp.logical_not(last_box), (SUBS, LANES))
    before_exists = jnp.broadcast_to(position > 0, (SUBS, LANES))

    def exists(q):
        return before_exists if q < 2 else None if q < 18 else after_exists

    def getter(stage):
        def get(ct, q, j):
            if q - 2 in INNER[stage]:
                return inner_ref[stage, ct, q - 2, j]
            return value_ref[stage, ct, q, j]

        return get

    def putter(stage):
        def put(ct, q, j, value):
            value_ref[stage, ct, q, j] = value

        return put

    def rest(stage, begin, end):
        return [q for q in range(begin, end) if q - 2 not in INNER[stage]]

    zero = jnp.zeros((SUBS, LANES), F32)
    for q in sorted(set(rest(0, 0, 28)) | set(rest(2, 1, 27))):
        wanted = (0, 1) if q in (0, 27) else (0, 1, 2)
        source = source_of(q)
        work.invert(q, 0, source, exists(q), wanted)
        if q - 2 not in INNER[0]:
            for ct in range(3):
                for j in wanted:
                    value_ref[0, ct, q, j] = source(0, ct, j) * inverse_ref[0, ct, q, j]
    for q in (0, 27):
        for ct in range(3):
            value_ref[0, ct, q, 2] = zero
            for j in range(3):
                value_ref[1, ct, q, j] = zero

    for q in sorted(set(rest(1, 1, 27)) | set(rest(3, 2, 26))):
        work.invert(q, 1, source_of(q), exists(q))
    work.update(rest(1, 1, 27), 1, getter(0), putter(1), source_of)
    work.update(rest(2, 1, 27), 0, getter(1), putter(2), source_of)

    place = placer(placed_ref, start, work.even)
    for begin, end, boxes in ((2, 18, (0, 1)), (18, 26, (2,))):
        places = rest(3, begin, end)
        work.update(places, 1, getter(2), putter(3), source_of, (0, 1))
        for box in boxes:
            @pl.when((box >= start) & (box < start + box_count))
            def _():
                for q in places:
                    if (q - 2) // 8 == box:
                        for ct in range(3):
                            for j in range(2):
                                place(ct, q, j, getter(2)(ct, q, j), value_ref[3, ct, q, j])
                for copy in send(box - start):
                    copy.start()

    for k in range(MOST):
        for copy in send(k):
            copy.wait()


def in_vmem(count):
    return [pl.BlockSpec(memory_space=pltpu.VMEM)] * count


def on_device(sources, absorption, conductance, diffusivity, run_lengths):
    channels, planes, cells = sources.shape
    boxes, groups = lax.axis_size("boxes"), lax.axis_size("grp")
    pairs = planes // 2
    real = lambda *shape: jax.ShapeDtypeStruct(shape + (SUBS, LANES), F32)
    vmem = lambda *shape: pltpu.VMEM(shape + (SUBS, LANES), F32)
    params = pltpu.CompilerParams(vmem_limit_bytes=VMEM_LIMIT)
    own, plane, first, second, box = pl.pallas_call(
        pack_rims,
        out_shape=(
            real(2, 3, pairs, 2),
            real(2, 2, 2),
            real(2 * pairs + 2),
            real(2 * pairs + 2),
            real(96),
        ),
        in_specs=in_vmem(1),
        out_specs=tuple(in_vmem(5)),
        scratch_shapes=[pltpu.VMEM((2, channels + 2, planes, LANES), F32)],
        compiler_params=params,
    )(jnp.concatenate([sources, absorption[None], conductance[None]]))
    second = lax.ppermute(second, "grp", swap_pairs(groups, 1))
    first = lax.ppermute(first, "grp", swap_pairs(groups, 0))
    box = lax.ppermute(box, "boxes", [(i + 1, i) for i in range(boxes - 1)])
    rim, rim_plane, chip, far = pl.pallas_call(
        pack_faces,
        out_shape=(real(2, 3, pairs), real(2, 2), real(60), real(60)),
        in_specs=in_vmem(4),
        out_specs=tuple(in_vmem(4)),
        cost_estimate=pl.CostEstimate(flops=5_000_000_000, bytes_accessed=0, transcendentals=0),
        compiler_params=params,
    )(own, plane, second, first)
    chip = lax.ppermute(chip, "boxes", swap_pairs(boxes, 0))
    far = lax.ppermute(far, "boxes", swap_pairs(boxes, 1))
    smem = pl.BlockSpec(memory_space=pltpu.SMEM)
    placed_shape = (2, 3 * SUBS, MOST * BOX_X, LANES)
    inner, placed, shift = pl.pallas_call(
        smooth_inner,
        out_shape=(
            real(4, 3, pairs, 3),
            jax.ShapeDtypeStruct(placed_shape, F32),
            jax.ShapeDtypeStruct((2, 2 * LANES, 2 * LANES), jnp.bfloat16),
        ),
        in_specs=[smem, smem] + in_vmem(4),
        out_specs=tuple(in_vmem(3)),
        scratch_shapes=[
            pltpu.VMEM((2, 6, 3, pairs, LANES), F32),
            pltpu.VMEM((2, 3, pairs, LANES), F32),
            vmem(2, 3, pairs + 2, 3),
        ],
        compiler_params=params,
        cost_estimate=pl.CostEstimate(flops=2_000_000_000, bytes_accessed=0, transcendentals=0),
    )(run_lengths, diffusivity, own, plane, rim, rim_plane)
    correction, _ = pl.pallas_call(
        smooth_outer,
        out_shape=(
            jax.ShapeDtypeStruct((channels, MOST * BOX_X, cells), F32),
            jax.ShapeDtypeStruct(placed_shape, F32),
        ),
        in_specs=[smem, smem] + in_vmem(10),
        out_specs=(pl.BlockSpec(memory_space=pltpu.HBM), in_vmem(1)[0]),
        input_output_aliases={11: 1},
        scratch_shapes=[
            pltpu.VMEM((2, 6, 3, RING, LANES), F32),
            pltpu.VMEM((2, 3, RING, LANES), F32),
            vmem(2, 3, 28, 3),
            vmem(4, 3, 28, 3),
            vmem(2, 3, 8),
            vmem(2, 3, 8),
            pltpu.SemaphoreType.DMA((MOST, 2)),
        ],
        compiler_params=params,
    )(run_lengths, diffusivity, own, plane, rim, rim_plane, box, far, chip, inner, shift, placed)
    return correction


def solution(mesh):
    return jax.shard_map(
        on_device,
        mesh=mesh,
        in_specs=(P(None, "boxes", "grp"), P("boxes", "grp"), P("boxes", "grp"), P(), P()),
        out_specs=P(None, "boxes", "grp"),
        check_vma=False,
    )
```

```python
import jax
import jax.numpy as jnp
from jax import lax
from jax.experimental import pallas as pl
from jax.experimental.pallas import tpu as pltpu
from jax.sharding import PartitionSpec as P

BOX_X = 16
PLANE_Z = 16
OLD_DEV = 2
MOST = 3
LANES = 128
SUBS = 8
RING = 32
RIM = 64
VMEM_LIMIT = 40 * 1024 * 1024
F32 = jnp.float32


def swap_pairs(count, first):
    lower = range(first, count - 1, 2)
    return [(i, i + 1) for i in lower] + [(i + 1, i) for i in lower]


def lane_places(rows):
    lane = lax.broadcasted_iota(jnp.int32, (rows, LANES), 1)
    even = (lane + lane // PLANE_Z) % 2 == 0
    return lane, even


def roll(x, shift):
    return pltpu.roll(x, shift % LANES, 1) if shift % LANES else x


def pack_rim(red, black, lane, high):
    red_from, black_from = (LANES - 48, LANES - 32) if high else (0, 0)
    reds = [roll(x, to - red_from) for x, to in zip(red, (0, 64, 64))]
    first = jnp.where(lane < 64, reds[0], reds[1])
    first = jnp.where((lane >= 48) & (lane < 64), roll(black[2], 48 - black_from), first)
    first = jnp.where(lane >= 112, roll(black[2], 96 - black_from), first)
    second = jnp.where(lane < 64, roll(black[1], 32 - black_from), reds[2])
    second = jnp.where(lane < 32, roll(black[0], -black_from), second)
    return first, second


def unpack_rim(first, second, lane, high):
    red_to, black_to = (LANES - 48, LANES - 32) if high else (0, 0)
    red = [roll(first, red_to), roll(first, red_to - 64), roll(second, red_to - 64)]
    black = [roll(second, black_to), roll(second, black_to - 32)]
    black.append(jnp.where(lane < black_to + 16, roll(first, black_to - 48), roll(first, black_to - 96)))
    return red, black


def pack_halo(red, black, lane):
    gap = (lane >= 48) & (lane < 80)
    wide = (lane >= 32) & (lane < 96)
    return [
        jnp.where(gap, roll(black[2], 48), red[0]),
        jnp.where(gap, roll(black[2], -48), red[1]),
        red[2],
        jnp.where(wide, roll(black[1], 64), black[0]),
    ]


def unpack_halo(parts, lane):
    black = jnp.where(lane < 64, roll(parts[0], -48), roll(parts[1], 48))
    return parts[:3], [parts[3], roll(parts[3], 64), black]


def pack_rims(
    src_ref,
    own_ref, plane_ref, first_ref, second_ref, box_ref,
    tiles_ref,
):
    layers, planes, _ = src_ref.shape
    channels = layers - 2
    half = planes // 2
    for layer in range(layers):
        for j in range(2):
            lanes = pl.ds(j * LANES, LANES)
            tiles_ref[j, layer] = src_ref[layer, :, lanes]

    lane, even = lane_places(SUBS)
    even_group = lax.axis_index("grp") % 2 == 0
    flat = tiles_ref.reshape(2 * layers * planes, LANES)

    for p in range(half):
        reds, blacks = [], []
        for j in range(2):
            red, black = [], []
            for ct in range(3):
                row = (j * layers + ct * SUBS) * planes + 2 * p
                low = flat[pl.ds(row, SUBS, stride=planes)]
                high = flat[pl.ds(row + 1, SUBS, stride=planes)]
                red.append(jnp.where(even, low, high))
                black.append(jnp.where(even, high, low))
                own_ref[0, ct, p, j] = red[ct]
                own_ref[1, ct, p, j] = black[ct]
                if p < 8:
                    box_ref[(ct * 8 + p) * 2 + j] = red[ct]
                    box_ref[((3 + ct) * 8 + p) * 2 + j] = black[ct]
                if p in (8, 9):
                    near = int(p == 8)
                    box_ref[96 + ct * 6 + EDGE.index((0, near, j))] = red[ct]
                    if near:
                        box_ref[96 + ct * 6 + EDGE.index((1, near, j))] = black[ct]
            reds.append(red)
            blacks.append(black)
        low_rim = pack_rim(reds[0], blacks[0], lane, False)
        high_rim = pack_rim(reds[1], blacks[1], lane, True)
        for i in range(2):
            first_ref[2 * p + i] = jnp.where(even_group, high_rim[i], low_rim[i])
            second_ref[2 * p + i] = jnp.where(even_group, low_rim[i], high_rim[i])

    for q in range(2):
        compact = []
        for j in range(2):
            row = (j * layers + channels + 1) * planes + 16 * q
            low = flat[pl.ds(row, SUBS, stride=2)]
            high = flat[pl.ds(row + 1, SUBS, stride=2)]
            compact.append((jnp.where(even, low, high), jnp.where(even, high, low)))
            for colour in range(2):
                plane_ref[colour, j, q] = compact[j][colour]
        low_rim = jnp.where(lane < RIM, compact[0][0], roll(compact[0][1], RIM))
        high_rim = jnp.where(lane < RIM, roll(compact[1][0], RIM), compact[1][1])
        first_ref[2 * half + q] = jnp.where(even_group, high_rim, low_rim)
        second_ref[2 * half + q] = jnp.where(even_group, low_rim, high_rim)


def pack_faces(own_ref, plane_ref, first_ref, second_ref, rim_ref, rim_plane_ref, chip_ref, far_ref):
    pairs = own_ref.shape[2]
    lane, _ = lane_places(SUBS)
    low_half = lane < RIM
    even_group = lax.axis_index("grp") % 2 == 0
    even_box = lax.axis_index("boxes") % 2 == 0

    def sides(i):
        first, second = first_ref[i], second_ref[i]
        return jnp.where(even_group, first, second), jnp.where(even_group, second, first)

    def put(i, to_before, to_after):
        chip_ref[i] = jnp.where(even_box, to_after, to_before)
        far_ref[i] = jnp.where(even_box, to_before, to_after)

    for p in range(pairs):
        above, below = zip(*[sides(2 * p + i) for i in range(2)])
        above, below = unpack_rim(*above, lane, False), unpack_rim(*below, lane, True)
        reds, blacks = [], []
        for ct in range(3):
            reds.append(jnp.where(low_half, above[0][ct], below[0][ct]))
            blacks.append(jnp.where(low_half, above[1][ct], below[1][ct]))
            rim_ref[0, ct, p] = reds[ct]
            rim_ref[1, ct, p] = blacks[ct]
        if p < 8:
            for i, part in enumerate(pack_halo(reds, blacks, lane)):
                k = 4 * p + i
                if k < 18:
                    colour, near, j = EDGE[k % 6]
                    put(k, part, own_ref[colour, k // 6, 15 if near else 14, j])
                else:
                    put(k, part, part)
    for q in range(2):
        above, below = sides(2 * pairs + q)
        rim_plane_ref[0, q] = jnp.where(low_half, above, roll(below, RIM))
        rim_plane_ref[1, q] = jnp.where(low_half, roll(above, RIM), below)

    for colour in range(2):
        for ct in range(3):
            put(32 + ct * 2 + colour, rim_ref[colour, ct, 8], rim_ref[colour, ct, 15])
        put(38 + colour, rim_plane_ref[colour, 0], rim_plane_ref[colour, 0])
    for colour in range(2):
        for near in range(2):
            for j in range(3):
                down, up = (0, 7) if near else (1, 6)
                rows = [
                    (plane_ref[colour, j, 1] if j < 2 else rim_plane_ref[colour, 1])[k : k + 1]
                    for k in (down, up)
                ]
                k = colour * 6 + near * 3 + j
                chip_ref[40 + k // 8, k % 8 : k % 8 + 1] = jnp.where(even_box, rows[1], rows[0])
                far_ref[40 + k // 8, k % 8 : k % 8 + 1] = jnp.where(even_box, rows[0], rows[1])
    chip_ref[41, 4:8] = jnp.zeros((4, LANES), F32)
    far_ref[41, 4:8] = jnp.zeros((4, LANES), F32)


EDGE = [(0, 1, 0), (0, 1, 1), (0, 0, 0), (0, 0, 1), (1, 1, 0), (1, 1, 1), (0, 1, 2), (1, 1, 2)]


def shift_matrices():
    row = lax.broadcasted_iota(jnp.int32, (2 * LANES, LANES), 0) % LANES
    col = lax.broadcasted_iota(jnp.int32, (2 * LANES, LANES), 1)
    z = col % PLANE_Z
    pick = lambda source: jnp.where(row == source, 1.0, 0.0)
    along_z = [pick(col - z + (z + step) % PLANE_Z) for step in (1, PLANE_Z - 1)]
    along_y = [pick((col + step) % LANES) for step in (PLANE_Z, LANES - PLANE_Z)]
    return [jnp.concatenate(pair, 1).astype(jnp.bfloat16) for pair in (along_z, along_y)]


def z_up(x, z):
    return jnp.where(z == PLANE_Z - 1, roll(x, PLANE_Z - 1), roll(x, -1))


def z_down(x, z):
    return jnp.where(z == 0, roll(x, 1 - PLANE_Z), roll(x, 1))


def lane_neighbours(tiles, lane, wanted=(0, 1, 2)):
    z = lane % PLANE_Z
    up = [roll(x, -PLANE_Z) for x in tiles]
    down = [roll(x, PLANE_Z) for x in tiles]
    return [
        [
            z_up(tiles[j], z),
            z_down(tiles[j], z),
            jnp.where(lane < LANES - PLANE_Z, up[j], up[(j + 1) % 3]),
            jnp.where(lane < PLANE_Z, down[(j + 2) % 3], down[j]),
        ]
        for j in wanted
    ]


INNER = [range(1, 15), range(1, 15), range(2, 14), range(2, 14)]


class Smoother:
    def __init__(self, factor_ref, face_ref, weight_ref, inverse_ref, shift_ref, channels, ring):
        self.face_ref, self.weight_ref, self.inverse_ref = face_ref, weight_ref, inverse_ref
        self.shift_ref, self.ring = shift_ref, ring
        self.lane, self.even = lane_places(SUBS)
        sub = lax.broadcasted_iota(jnp.int32, (SUBS, LANES), 0)
        group = lax.axis_index("grp")
        above = jnp.where(group == lax.axis_size("grp") - 1, 0, LANES)
        below = jnp.where(group == 0, LANES, 0)
        self.limit = [
            ((self.lane < jnp.minimum(above, PLANE_Z * rows)))
            | (self.lane >= jnp.maximum(below, LANES - PLANE_Z * rows))
            for rows in (3, 2)
        ]
        self.factors = []
        for ct in range(3):
            factor = jnp.zeros((SUBS, LANES), F32)
            for i in range(min(SUBS, channels - ct * SUBS)):
                factor = jnp.where(sub == i, 0.5 * factor_ref[ct * SUBS + i], factor)
            self.factors.append(factor)

    def find_faces(self, conduct):
        wide_lane, wide_even = lane_places(self.ring)
        for colour in range(2):
            others = conduct[1 - colour]
            beside = lane_neighbours(others, wide_lane)
            for j in range(3):
                after, before = pltpu.roll(others[j], self.ring - 1, 0), pltpu.roll(others[j], 1, 0)
                across = jnp.where(wide_even, *((before, after) if colour == 0 else (after, before)))
                total = jnp.zeros((self.ring, LANES), F32)
                for i, other in enumerate([others[j], across] + beside[j]):
                    face = conduct[colour][j] + other
                    self.face_ref[colour, i, j] = face
                    total = total + face
                self.weight_ref[colour, j] = total

    def spread(self, ref, index, q):
        row = (q + RING - 2) % RING
        return jnp.broadcast_to(ref[index + (pl.ds(row, 1),)], (SUBS, LANES))

    def invert(self, q, colour, source, exists, wanted=(0, 1, 2)):
        for j in wanted:
            absorb = jnp.broadcast_to(source(colour, 2, j)[6:7], (SUBS, LANES))
            weight = self.spread(self.weight_ref, (colour, j), q)
            keep = exists if j < 2 else self.limit[colour]
            if exists is not None and j == 2:
                keep = keep & exists
            for ct in range(3):
                inverse = 1.0 / (absorb + self.factors[ct] * weight)
                if keep is not None:
                    inverse = jnp.where(keep, inverse, 0.0)
                self.inverse_ref[colour, ct, q, j] = inverse

    def shifted(self, places, get):
        index = [(ct, q, j) for q in places for ct in range(3) for j in range(3)]
        x = jnp.concatenate([get(*key) for key in index], 0)
        high = x.astype(jnp.bfloat16)
        both = jnp.concatenate([high, (x - high.astype(F32)).astype(jnp.bfloat16)], 1)
        moved = [jnp.dot(both, self.shift_ref[i], preferred_element_type=F32) for i in range(2)]
        result = {}
        for k, key in enumerate(index):
            rows = slice(k * SUBS, (k + 1) * SUBS)
            result[key] = [m[rows, i * LANES : (i + 1) * LANES] for m in moved for i in range(2)]
        return result

    def update(self, places, colour, get, put, source_of, wanted=(0, 1, 2)):
        lane, even = self.lane, self.even
        moved = self.shifted(places, get)
        for q in places:
            source = source_of(q)
            faces = [
                [self.spread(self.face_ref, (colour, i, j), q) for i in range(6)] for j in wanted
            ]
            for ct in range(3):
                near = [moved[ct, q, j] for j in range(3)]
                for j, face in zip(wanted, faces):
                    before, after = get(ct, q - 1, j), get(ct, q + 1, j)
                    across = jnp.where(even, *((before, after) if colour == 0 else (after, before)))
                    up = jnp.where(lane < LANES - PLANE_Z, near[j][2], near[(j + 1) % 3][2])
                    down = jnp.where(lane < PLANE_Z, near[(j + 2) % 3][3], near[j][3])
                    inflow = face[0] * get(ct, q, j)
                    for one, other in zip(face[1:], [across, near[j][0], near[j][1], up, down]):
                        inflow = inflow + one * other
                    value = source(colour, ct, j) + self.factors[ct] * inflow
                    put(ct, q, j, value * self.inverse_ref[colour, ct, q, j])


def own_run(lengths_ref):
    position = lax.axis_index("boxes")
    first_box = lax.fori_loop(0, position, lambda i, total: total + lengths_ref[i], jnp.int32(0))
    return first_box - position * OLD_DEV, lengths_ref[position]


def placer(placed_ref, start, even):
    rows = placed_ref.shape[2]
    flat = placed_ref.reshape(2 * 3 * SUBS * rows, LANES)

    def place(ct, q, j, red, black):
        row = (j * 3 + ct) * SUBS * rows + 2 * (q - 2 - 8 * start)
        flat[pl.ds(row, SUBS, stride=rows)] = jnp.where(even, red, black)
        flat[pl.ds(row + 1, SUBS, stride=rows)] = jnp.where(even, black, red)

    return place


def smooth_inner(
    lengths_ref, factor_ref, own_ref, plane_ref, rim_ref, rim_plane_ref,
    value_ref, placed_ref, shift_ref,
    face_ref, weight_ref, inverse_ref,
):
    pairs = own_ref.shape[2]
    channels = factor_ref.shape[0]
    work = Smoother(factor_ref, face_ref, weight_ref, inverse_ref, shift_ref, channels, pairs)
    for i, matrix in enumerate(shift_matrices()):
        shift_ref[i] = matrix

    def plane(colour, j):
        return [plane_ref[colour, j, k] if j < 2 else rim_plane_ref[colour, k] for k in range(2)]

    work.find_faces(
        [[jnp.concatenate(plane(colour, j), 0) for j in range(3)] for colour in range(2)]
    )

    def source_of(q):
        p = q - 2
        return lambda colour, ct, j: own_ref[colour, ct, p, j] if j < 2 else rim_ref[colour, ct, p]

    def getter(stage):
        return lambda ct, q, j: value_ref[stage, ct, q - 2, j]

    def putter(stage):
        def put(ct, q, j, value):
            value_ref[stage, ct, q - 2, j] = value

        return put

    for p in range(pairs):
        source = source_of(p + 2)
        work.invert(p + 2, 0, source, None)
        work.invert(p + 2, 1, source, None)
        for ct in range(3):
            for j in range(3):
                value_ref[0, ct, p, j] = source(0, ct, j) * inverse_ref[0, ct, p + 2, j]
    for p in (0, pairs - 1):
        for ct in range(3):
            for j in range(3):
                value_ref[1, ct, p, j] = jnp.zeros((SUBS, LANES), F32)
    for places in (range(3, 11), range(11, 17)):
        work.update(places, 1, getter(0), putter(1), source_of)
    for places in (range(3, 11), range(11, 17)):
        work.update(places, 0, getter(1), putter(2), source_of)
    for places in (range(4, 10), range(10, 16)):
        work.update(places, 1, getter(2), putter(3), source_of, (0, 1))

    start, box_count = own_run(lengths_ref)
    place = placer(placed_ref, start, work.even)
    for box, places in enumerate((range(4, 10), range(10, 16))):
        @pl.when((box >= start) & (box < start + box_count))
        def _():
            for q in places:
                for ct in range(3):
                    for j in range(2):
                        place(ct, q, j, getter(2)(ct, q, j), getter(3)(ct, q, j))

    for k in range(1, MOST):
        @pl.when(k >= box_count)
        def _():
            for j in range(2):
                for c in range(channels):
                    placed_ref[j, c, k * BOX_X : (k + 1) * BOX_X] = jnp.zeros((BOX_X, LANES), F32)


def smooth_outer(
    lengths_ref, factor_ref, own_ref, plane_ref, rim_ref, rim_plane_ref, box_ref, far_ref, chip_ref,
    inner_ref, shift_ref, given_ref,
    out_ref, placed_ref,
    face_ref, weight_ref, inverse_ref, value_ref, box_rim_ref, edge_ref, sems,
):
    channels = out_ref.shape[0]
    position = lax.axis_index("boxes")
    even_box = position % 2 == 0
    last_box = position == lax.axis_size("boxes") - 1
    work = Smoother(factor_ref, face_ref, weight_ref, inverse_ref, shift_ref, channels, RING)
    lane = work.lane
    sub = lax.broadcasted_iota(jnp.int32, (SUBS, LANES), 0)
    start, box_count = own_run(lengths_ref)

    def send(k):
        rows = pl.ds(pl.multiple_of(k * BOX_X, BOX_X), BOX_X)
        return [
            pltpu.make_async_copy(
                placed_ref.at[j, pl.ds(0, channels), rows],
                out_ref.at[:, rows, pl.ds(j * LANES, LANES)],
                sems.at[k, j],
            )
            for j in range(2)
        ]

    for k in range(1, MOST):
        @pl.when(k >= box_count)
        def _():
            for copy in send(k):
                copy.start()

    def from_after(i):
        return jnp.where(even_box, chip_ref[i], far_ref[i])

    def from_before(i):
        return jnp.where(even_box, far_ref[i], chip_ref[i])

    edges = [jnp.concatenate([get(40), get(41)], 0) for get in (from_after, from_before)]
    flat_box = box_ref.reshape(114 * SUBS, LANES)
    conduct = []
    for colour in range(2):
        planes = []
        for j in range(3):
            own = [plane_ref[colour, j, k] if j < 2 else rim_plane_ref[colour, k] for k in range(2)]
            if j < 2:
                row = (((3 * colour + 2) * 8) * 2 + j) * SUBS + 7
                box = flat_box[pl.ds(row, SUBS, stride=2 * SUBS)]
            else:
                box = from_after(38 + colour)
            edge = jnp.zeros((SUBS, LANES), F32)
            for place_at, side, near in ((0, 0, 1), (1, 0, 0), (6, 1, 0), (7, 1, 1)):
                k = colour * 6 + near * 3 + j
                row = jnp.broadcast_to(edges[side][k : k + 1], (SUBS, LANES))
                edge = jnp.where(sub == place_at, row, edge)
            planes.append(jnp.concatenate(own + [box, edge], 0))
        conduct.append(planes)
    work.find_faces(conduct)

    for p in range(8):
        reds, blacks = unpack_halo([from_after(4 * p + i) for i in range(4)], lane)
        for ct in range(3):
            box_rim_ref[0, ct, p], box_rim_ref[1, ct, p] = reds[ct], blacks[ct]
    for ct in range(3):
        for i in range(6):
            edge_ref[0, ct, i] = from_before(ct * 6 + i)
            edge_ref[1, ct, i] = box_ref[96 + ct * 6 + i]
        for colour in range(2):
            edge_ref[0, ct, 6 + colour] = from_before(32 + ct * 2 + colour)
            edge_ref[1, ct, 6 + colour] = from_after(32 + ct * 2 + colour)

    def source_of(q):
        if 2 <= q < 18:
            return lambda colour, ct, j: (
                own_ref[colour, ct, q - 2, j] if j < 2 else rim_ref[colour, ct, q - 2]
            )
        if 18 <= q < 26:
            return lambda colour, ct, j: (
                box_ref[((colour * 3 + ct) * 8 + q - 18) * 2 + j]
                if j < 2
                else box_rim_ref[colour, ct, q - 18]
            )
        near, side = int(q in (1, 26)), int(q > 20)
        return lambda colour, ct, j: edge_ref[side, ct, EDGE.index((colour, near, j))]

    after_exists = jnp.broadcast_to(jnp.logical_not(last_box), (SUBS, LANES))
    before_exists = jnp.broadcast_to(position > 0, (SUBS, LANES))

    def exists(q):
        return before_exists if q < 2 else None if q < 18 else after_exists

    def getter(stage):
        def get(ct, q, j):
            if q - 2 in INNER[stage]:
                return inner_ref[stage, ct, q - 2, j]
            return value_ref[stage, ct, q, j]

        return get

    def putter(stage):
        def put(ct, q, j, value):
            value_ref[stage, ct, q, j] = value

        return put

    def rest(stage, begin, end):
        return [q for q in range(begin, end) if q - 2 not in INNER[stage]]

    zero = jnp.zeros((SUBS, LANES), F32)
    for q in sorted(set(rest(0, 0, 28)) | set(rest(2, 1, 27))):
        wanted = (0, 1) if q in (0, 27) else (0, 1, 2)
        source = source_of(q)
        work.invert(q, 0, source, exists(q), wanted)
        if q - 2 not in INNER[0]:
            for ct in range(3):
                for j in wanted:
                    value_ref[0, ct, q, j] = source(0, ct, j) * inverse_ref[0, ct, q, j]
    for q in (0, 27):
        for ct in range(3):
            value_ref[0, ct, q, 2] = zero
            for j in range(3):
                value_ref[1, ct, q, j] = zero

    for q in sorted(set(rest(1, 1, 27)) | set(rest(3, 2, 26))):
        work.invert(q, 1, source_of(q), exists(q))
    work.update(rest(1, 1, 27), 1, getter(0), putter(1), source_of)
    work.update(rest(2, 1, 27), 0, getter(1), putter(2), source_of)

    place = placer(placed_ref, start, work.even)
    for begin, end, boxes in ((2, 18, (0, 1)), (18, 26, (2,))):
        places = rest(3, begin, end)
        work.update(places, 1, getter(2), putter(3), source_of, (0, 1))
        for box in boxes:
            @pl.when((box >= start) & (box < start + box_count))
            def _():
                for q in places:
                    if (q - 2) // 8 == box:
                        for ct in range(3):
                            for j in range(2):
                                place(ct, q, j, getter(2)(ct, q, j), value_ref[3, ct, q, j])
                for copy in send(box - start):
                    copy.start()

    for k in range(MOST):
        for copy in send(k):
            copy.wait()


def in_vmem(count):
    return [pl.BlockSpec(memory_space=pltpu.VMEM)] * count


def on_device(sources, absorption, conductance, diffusivity, run_lengths):
    channels, planes, cells = sources.shape
    boxes, groups = lax.axis_size("boxes"), lax.axis_size("grp")
    pairs = planes // 2
    real = lambda *shape: jax.ShapeDtypeStruct(shape + (SUBS, LANES), F32)
    vmem = lambda *shape: pltpu.VMEM(shape + (SUBS, LANES), F32)
    params = pltpu.CompilerParams(vmem_limit_bytes=VMEM_LIMIT)
    own, plane, first, second, box = pl.pallas_call(
        pack_rims,
        out_shape=(
            real(2, 3, pairs, 2),
            real(2, 2, 2),
            real(2 * pairs + 2),
            real(2 * pairs + 2),
            real(114),
        ),
        in_specs=in_vmem(1),
        out_specs=tuple(in_vmem(5)),
        scratch_shapes=[pltpu.VMEM((2, channels + 2, planes, LANES), F32)],
        compiler_params=params,
    )(jnp.concatenate([sources, absorption[None], conductance[None]]))
    second = lax.ppermute(second, "grp", swap_pairs(groups, 1))
    first = lax.ppermute(first, "grp", swap_pairs(groups, 0))
    box = lax.ppermute(box, "boxes", [(i + 1, i) for i in range(boxes - 1)])
    rim, rim_plane, chip, far = pl.pallas_call(
        pack_faces,
        out_shape=(real(2, 3, pairs), real(2, 2), real(42), real(42)),
        in_specs=in_vmem(4),
        out_specs=tuple(in_vmem(4)),
        cost_estimate=pl.CostEstimate(flops=5_000_000_000, bytes_accessed=0, transcendentals=0),
        compiler_params=params,
    )(own, plane, first, second)
    chip = lax.ppermute(chip, "boxes", swap_pairs(boxes, 0))
    far = lax.ppermute(far, "boxes", swap_pairs(boxes, 1))
    smem = pl.BlockSpec(memory_space=pltpu.SMEM)
    placed_shape = (2, 3 * SUBS, MOST * BOX_X, LANES)
    inner, placed, shift = pl.pallas_call(
        smooth_inner,
        out_shape=(
            real(4, 3, pairs, 3),
            jax.ShapeDtypeStruct(placed_shape, F32),
            jax.ShapeDtypeStruct((2, 2 * LANES, 2 * LANES), jnp.bfloat16),
        ),
        in_specs=[smem, smem] + in_vmem(4),
        out_specs=tuple(in_vmem(3)),
        scratch_shapes=[
            pltpu.VMEM((2, 6, 3, pairs, LANES), F32),
            pltpu.VMEM((2, 3, pairs, LANES), F32),
            vmem(2, 3, pairs + 2, 3),
        ],
        compiler_params=params,
        cost_estimate=pl.CostEstimate(flops=2_000_000_000, bytes_accessed=0, transcendentals=0),
    )(run_lengths, diffusivity, own, plane, rim, rim_plane)
    correction, _ = pl.pallas_call(
        smooth_outer,
        out_shape=(
            jax.ShapeDtypeStruct((channels, MOST * BOX_X, cells), F32),
            jax.ShapeDtypeStruct(placed_shape, F32),
        ),
        in_specs=[smem, smem] + in_vmem(10),
        out_specs=(pl.BlockSpec(memory_space=pltpu.HBM), in_vmem(1)[0]),
        input_output_aliases={11: 1},
        scratch_shapes=[
            pltpu.VMEM((2, 6, 3, RING, LANES), F32),
            pltpu.VMEM((2, 3, RING, LANES), F32),
            vmem(2, 3, 28, 3),
            vmem(4, 3, 28, 3),
            vmem(2, 3, 8),
            vmem(2, 3, 8),
            pltpu.SemaphoreType.DMA((MOST, 2)),
        ],
        compiler_params=params,
    )(run_lengths, diffusivity, own, plane, rim, rim_plane, box, far, chip, inner, shift, placed)
    return correction


def solution(mesh):
    return jax.shard_map(
        on_device,
        mesh=mesh,
        in_specs=(P(None, "boxes", "grp"), P("boxes", "grp"), P("boxes", "grp"), P(), P()),
        out_specs=P(None, "boxes", "grp"),
        check_vma=False,
    )
```

```python
import jax
import jax.numpy as jnp
from jax import lax
from jax.experimental import pallas as pl
from jax.experimental.pallas import tpu as pltpu
from jax.sharding import PartitionSpec as P

BOX_X = 16
PLANE_Z = 16
OLD_DEV = 2
MOST = 3
LANES = 128
SUBS = 8
RING = 32
RIM = 64
VMEM_LIMIT = 40 * 1024 * 1024
F32 = jnp.float32


def swap_pairs(boxes, groups, along_boxes, first):
    count, other = (boxes, groups) if along_boxes else (groups, boxes)
    pairs = []
    for i in range(count):
        k = i + 1 if (i - first) % 2 == 0 else i - 1
        for m in range(other):
            here, there = (i, m), (k, m)
            if not 0 <= k < count:
                there = (i, m ^ 1)
                if (m ^ 1) >= other:
                    continue
            if not along_boxes:
                here, there = here[::-1], there[::-1]
            pairs.append(tuple(b * groups + g for b, g in (here, there)))
    return pairs


def lane_places(rows):
    lane = lax.broadcasted_iota(jnp.int32, (rows, LANES), 1)
    even = (lane + lane // PLANE_Z) % 2 == 0
    return lane, even


def roll(x, shift):
    return pltpu.roll(x, shift % LANES, 1) if shift % LANES else x


def pack_rim(red, black, lane, high):
    red_from, black_from = (LANES - 48, LANES - 32) if high else (0, 0)
    reds = [roll(x, to - red_from) for x, to in zip(red, (0, 64, 64))]
    first = jnp.where(lane < 64, reds[0], reds[1])
    first = jnp.where((lane >= 48) & (lane < 64), roll(black[2], 48 - black_from), first)
    first = jnp.where(lane >= 112, roll(black[2], 96 - black_from), first)
    second = jnp.where(lane < 64, roll(black[1], 32 - black_from), reds[2])
    second = jnp.where(lane < 32, roll(black[0], -black_from), second)
    return first, second


def unpack_rim(first, second, lane, high):
    red_to, black_to = (LANES - 48, LANES - 32) if high else (0, 0)
    red = [roll(first, red_to), roll(first, red_to - 64), roll(second, red_to - 64)]
    black = [roll(second, black_to), roll(second, black_to - 32)]
    black.append(jnp.where(lane < black_to + 16, roll(first, black_to - 48), roll(first, black_to - 96)))
    return red, black


def pack_halo(red, black, lane):
    gap = (lane >= 48) & (lane < 80)
    wide = (lane >= 32) & (lane < 96)
    return [
        jnp.where(gap, roll(black[2], 48), red[0]),
        jnp.where(gap, roll(black[2], -48), red[1]),
        red[2],
        jnp.where(wide, roll(black[1], 64), black[0]),
    ]


def unpack_halo(parts, lane):
    black = jnp.where(lane < 64, roll(parts[0], -48), roll(parts[1], 48))
    return parts[:3], [parts[3], roll(parts[3], 64), black]


def pack_rims(
    src_ref,
    own_ref, plane_ref, first_ref, second_ref, box_ref,
    tiles_ref,
):
    layers, planes, _ = src_ref.shape
    channels = layers - 2
    half = planes // 2
    for layer in range(layers):
        for j in range(2):
            lanes = pl.ds(j * LANES, LANES)
            tiles_ref[j, layer] = src_ref[layer, :, lanes]

    lane, even = lane_places(SUBS)
    even_group = lax.axis_index("grp") % 2 == 0
    flat = tiles_ref.reshape(2 * layers * planes, LANES)

    for p in range(half):
        reds, blacks = [], []
        for j in range(2):
            red, black = [], []
            for ct in range(3):
                row = (j * layers + ct * SUBS) * planes + 2 * p
                low = flat[pl.ds(row, SUBS, stride=planes)]
                high = flat[pl.ds(row + 1, SUBS, stride=planes)]
                red.append(jnp.where(even, low, high))
                black.append(jnp.where(even, high, low))
                own_ref[0, ct, p, j] = red[ct]
                own_ref[1, ct, p, j] = black[ct]
                if p < 8:
                    box_ref[(ct * 8 + p) * 2 + j] = red[ct]
                    box_ref[((3 + ct) * 8 + p) * 2 + j] = black[ct]
                if p in (8, 9):
                    near = int(p == 8)
                    box_ref[96 + ct * 6 + EDGE.index((0, near, j))] = red[ct]
                    if near:
                        box_ref[96 + ct * 6 + EDGE.index((1, near, j))] = black[ct]
            reds.append(red)
            blacks.append(black)
        low_rim = pack_rim(reds[0], blacks[0], lane, False)
        high_rim = pack_rim(reds[1], blacks[1], lane, True)
        for i in range(2):
            first_ref[2 * p + i] = jnp.where(even_group, high_rim[i], low_rim[i])
            second_ref[2 * p + i] = jnp.where(even_group, low_rim[i], high_rim[i])

    for q in range(2):
        compact = []
        for j in range(2):
            row = (j * layers + channels + 1) * planes + 16 * q
            low = flat[pl.ds(row, SUBS, stride=2)]
            high = flat[pl.ds(row + 1, SUBS, stride=2)]
            compact.append((jnp.where(even, low, high), jnp.where(even, high, low)))
            for colour in range(2):
                plane_ref[colour, j, q] = compact[j][colour]
        low_rim = jnp.where(lane < RIM, compact[0][0], roll(compact[0][1], RIM))
        high_rim = jnp.where(lane < RIM, roll(compact[1][0], RIM), compact[1][1])
        first_ref[2 * half + q] = jnp.where(even_group, high_rim, low_rim)
        second_ref[2 * half + q] = jnp.where(even_group, low_rim, high_rim)


def pack_faces(own_ref, plane_ref, first_ref, second_ref, rim_ref, rim_plane_ref, chip_ref, far_ref):
    pairs = own_ref.shape[2]
    lane, _ = lane_places(SUBS)
    low_half = lane < RIM
    group = lax.axis_index("grp")
    even_group = group % 2 == 0
    even_box = lax.axis_index("boxes") % 2 == 0

    def sides(i):
        first, second = first_ref[i], second_ref[i]
        return jnp.where(even_group, first, second), jnp.where(even_group, second, first)

    def put(i, to_before, to_after):
        chip_ref[i] = jnp.where(even_box, to_after, to_before)
        far_ref[i] = jnp.where(even_box, to_before, to_after)

    for p in range(pairs):
        above, below = zip(*[sides(2 * p + i) for i in range(2)])
        above, below = unpack_rim(*above, lane, False), unpack_rim(*below, lane, True)
        reds, blacks = [], []
        for ct in range(3):
            reds.append(jnp.where(low_half, above[0][ct], below[0][ct]))
            blacks.append(jnp.where(low_half, above[1][ct], below[1][ct]))
            rim_ref[0, ct, p] = reds[ct]
            rim_ref[1, ct, p] = blacks[ct]
        if p < 8:
            for i, part in enumerate(pack_halo(reds, blacks, lane)):
                k = 4 * p + i
                if k < 18:
                    colour, near, j = EDGE[k % 6]
                    put(k, part, own_ref[colour, k // 6, 15 if near else 14, j])
                else:
                    put(k, part, part)
    for q in range(2):
        above, below = sides(2 * pairs + q)
        above = jnp.where(group == lax.axis_size("grp") - 1, 0.0, above)
        below = jnp.where(group == 0, 0.0, below)
        rim_plane_ref[0, q] = jnp.where(low_half, above, roll(below, RIM))
        rim_plane_ref[1, q] = jnp.where(low_half, roll(above, RIM), below)

    for colour in range(2):
        for ct in range(3):
            put(32 + ct * 2 + colour, rim_ref[colour, ct, 8], rim_ref[colour, ct, 15])
        put(38 + colour, rim_plane_ref[colour, 0], rim_plane_ref[colour, 0])
    for colour in range(2):
        for near in range(2):
            for j in range(3):
                down, up = (0, 7) if near else (1, 6)
                rows = [
                    (plane_ref[colour, j, 1] if j < 2 else rim_plane_ref[colour, 1])[k : k + 1]
                    for k in (down, up)
                ]
                k = colour * 6 + near * 3 + j
                chip_ref[40 + k // 8, k % 8 : k % 8 + 1] = jnp.where(even_box, rows[1], rows[0])
                far_ref[40 + k // 8, k % 8 : k % 8 + 1] = jnp.where(even_box, rows[0], rows[1])
    chip_ref[41, 4:8] = jnp.zeros((4, LANES), F32)
    far_ref[41, 4:8] = jnp.zeros((4, LANES), F32)


EDGE = [(0, 1, 0), (0, 1, 1), (0, 0, 0), (0, 0, 1), (1, 1, 0), (1, 1, 1), (0, 1, 2), (1, 1, 2)]


def shift_matrices():
    row = lax.broadcasted_iota(jnp.int32, (2 * LANES, LANES), 0) % LANES
    col = lax.broadcasted_iota(jnp.int32, (2 * LANES, LANES), 1)
    z = col % PLANE_Z
    pick = lambda source: jnp.where(row == source, 1.0, 0.0)
    along_z = [pick(col - z + (z + step) % PLANE_Z) for step in (1, PLANE_Z - 1)]
    along_y = [pick((col + step) % LANES) for step in (PLANE_Z, LANES - PLANE_Z)]
    return [jnp.concatenate(pair, 1).astype(jnp.bfloat16) for pair in (along_z, along_y)]


def z_up(x, z):
    return jnp.where(z == PLANE_Z - 1, roll(x, PLANE_Z - 1), roll(x, -1))


def z_down(x, z):
    return jnp.where(z == 0, roll(x, 1 - PLANE_Z), roll(x, 1))


def lane_neighbours(tiles, lane, wanted=(0, 1, 2)):
    z = lane % PLANE_Z
    up = [roll(x, -PLANE_Z) for x in tiles]
    down = [roll(x, PLANE_Z) for x in tiles]
    return [
        [
            z_up(tiles[j], z),
            z_down(tiles[j], z),
            jnp.where(lane < LANES - PLANE_Z, up[j], up[(j + 1) % 3]),
            jnp.where(lane < PLANE_Z, down[(j + 2) % 3], down[j]),
        ]
        for j in wanted
    ]


INNER = [range(1, 15), range(1, 15), range(2, 14), range(2, 14)]


class Smoother:
    def __init__(self, factor_ref, face_ref, weight_ref, inverse_ref, shift_ref, channels, ring):
        self.face_ref, self.weight_ref, self.inverse_ref = face_ref, weight_ref, inverse_ref
        self.shift_ref, self.ring = shift_ref, ring
        self.lane, self.even = lane_places(SUBS)
        sub = lax.broadcasted_iota(jnp.int32, (SUBS, LANES), 0)
        group = lax.axis_index("grp")
        above = jnp.where(group == lax.axis_size("grp") - 1, 0, LANES)
        below = jnp.where(group == 0, LANES, 0)
        self.limit = [
            ((self.lane < jnp.minimum(above, PLANE_Z * rows)))
            | (self.lane >= jnp.maximum(below, LANES - PLANE_Z * rows))
            for rows in (3, 2)
        ]
        self.factors = []
        for ct in range(3):
            factor = jnp.zeros((SUBS, LANES), F32)
            for i in range(min(SUBS, channels - ct * SUBS)):
                factor = jnp.where(sub == i, 0.5 * factor_ref[ct * SUBS + i], factor)
            self.factors.append(factor)

    def find_faces(self, conduct):
        wide_lane, wide_even = lane_places(self.ring)
        for colour in range(2):
            others = conduct[1 - colour]
            beside = lane_neighbours(others, wide_lane)
            for j in range(3):
                after, before = pltpu.roll(others[j], self.ring - 1, 0), pltpu.roll(others[j], 1, 0)
                across = jnp.where(wide_even, *((before, after) if colour == 0 else (after, before)))
                total = jnp.zeros((self.ring, LANES), F32)
                for i, other in enumerate([others[j], across] + beside[j]):
                    face = conduct[colour][j] + other
                    self.face_ref[colour, i, j] = face
                    total = total + face
                self.weight_ref[colour, j] = total

    def spread(self, ref, index, q):
        row = (q + RING - 2) % RING
        return jnp.broadcast_to(ref[index + (pl.ds(row, 1),)], (SUBS, LANES))

    def invert(self, q, colour, source, exists, wanted=(0, 1, 2)):
        for j in wanted:
            absorb = jnp.broadcast_to(source(colour, 2, j)[6:7], (SUBS, LANES))
            weight = self.spread(self.weight_ref, (colour, j), q)
            keep = exists if j < 2 else self.limit[colour]
            if exists is not None and j == 2:
                keep = keep & exists
            for ct in range(3):
                inverse = 1.0 / (absorb + self.factors[ct] * weight)
                if keep is not None:
                    inverse = jnp.where(keep, inverse, 0.0)
                self.inverse_ref[colour, ct, q, j] = inverse

    def shifted(self, places, get):
        index = [(ct, q, j) for q in places for ct in range(3) for j in range(3)]
        x = jnp.concatenate([get(*key) for key in index], 0)
        high = x.astype(jnp.bfloat16)
        both = jnp.concatenate([high, (x - high.astype(F32)).astype(jnp.bfloat16)], 1)
        moved = [jnp.dot(both, self.shift_ref[i], preferred_element_type=F32) for i in range(2)]
        result = {}
        for k, key in enumerate(index):
            rows = slice(k * SUBS, (k + 1) * SUBS)
            result[key] = [m[rows, i * LANES : (i + 1) * LANES] for m in moved for i in range(2)]
        return result

    def update(self, places, colour, get, put, source_of, wanted=(0, 1, 2)):
        lane, even = self.lane, self.even
        moved = self.shifted(places, get)
        for q in places:
            source = source_of(q)
            faces = [
                [self.spread(self.face_ref, (colour, i, j), q) for i in range(6)] for j in wanted
            ]
            for ct in range(3):
                near = [moved[ct, q, j] for j in range(3)]
                for j, face in zip(wanted, faces):
                    before, after = get(ct, q - 1, j), get(ct, q + 1, j)
                    across = jnp.where(even, *((before, after) if colour == 0 else (after, before)))
                    up = jnp.where(lane < LANES - PLANE_Z, near[j][2], near[(j + 1) % 3][2])
                    down = jnp.where(lane < PLANE_Z, near[(j + 2) % 3][3], near[j][3])
                    inflow = face[0] * get(ct, q, j)
                    for one, other in zip(face[1:], [across, near[j][0], near[j][1], up, down]):
                        inflow = inflow + one * other
                    value = source(colour, ct, j) + self.factors[ct] * inflow
                    put(ct, q, j, value * self.inverse_ref[colour, ct, q, j])


def own_run(lengths_ref):
    position = lax.axis_index("boxes")
    first_box = lax.fori_loop(0, position, lambda i, total: total + lengths_ref[i], jnp.int32(0))
    return first_box - position * OLD_DEV, lengths_ref[position]


def placer(placed_ref, start, even):
    rows = placed_ref.shape[2]
    flat = placed_ref.reshape(2 * 3 * SUBS * rows, LANES)

    def place(ct, q, j, red, black):
        row = (j * 3 + ct) * SUBS * rows + 2 * (q - 2 - 8 * start)
        flat[pl.ds(row, SUBS, stride=rows)] = jnp.where(even, red, black)
        flat[pl.ds(row + 1, SUBS, stride=rows)] = jnp.where(even, black, red)

    return place


def smooth_inner(
    lengths_ref, factor_ref, own_ref, plane_ref, rim_ref, rim_plane_ref,
    value_ref, placed_ref, shift_ref,
    face_ref, weight_ref, inverse_ref,
):
    pairs = own_ref.shape[2]
    channels = factor_ref.shape[0]
    work = Smoother(factor_ref, face_ref, weight_ref, inverse_ref, shift_ref, channels, pairs)
    for i, matrix in enumerate(shift_matrices()):
        shift_ref[i] = matrix

    def plane(colour, j):
        return [plane_ref[colour, j, k] if j < 2 else rim_plane_ref[colour, k] for k in range(2)]

    work.find_faces(
        [[jnp.concatenate(plane(colour, j), 0) for j in range(3)] for colour in range(2)]
    )

    def source_of(q):
        p = q - 2
        return lambda colour, ct, j: own_ref[colour, ct, p, j] if j < 2 else rim_ref[colour, ct, p]

    def getter(stage):
        return lambda ct, q, j: value_ref[stage, ct, q - 2, j]

    def putter(stage):
        def put(ct, q, j, value):
            value_ref[stage, ct, q - 2, j] = value

        return put

    for p in range(pairs):
        source = source_of(p + 2)
        work.invert(p + 2, 0, source, None)
        work.invert(p + 2, 1, source, None)
        for ct in range(3):
            for j in range(3):
                value_ref[0, ct, p, j] = source(0, ct, j) * inverse_ref[0, ct, p + 2, j]
    for p in (0, pairs - 1):
        for ct in range(3):
            for j in range(3):
                value_ref[1, ct, p, j] = jnp.zeros((SUBS, LANES), F32)
    for places in (range(3, 11), range(11, 17)):
        work.update(places, 1, getter(0), putter(1), source_of)
    for places in (range(3, 11), range(11, 17)):
        work.update(places, 0, getter(1), putter(2), source_of)
    for places in (range(4, 10), range(10, 16)):
        work.update(places, 1, getter(2), putter(3), source_of, (0, 1))

    start, box_count = own_run(lengths_ref)
    place = placer(placed_ref, start, work.even)
    for box, places in enumerate((range(4, 10), range(10, 16))):
        @pl.when((box >= start) & (box < start + box_count))
        def _():
            for q in places:
                for ct in range(3):
                    for j in range(2):
                        place(ct, q, j, getter(2)(ct, q, j), getter(3)(ct, q, j))

    for k in range(1, MOST):
        @pl.when(k >= box_count)
        def _():
            for j in range(2):
                for c in range(channels):
                    placed_ref[j, c, k * BOX_X : (k + 1) * BOX_X] = jnp.zeros((BOX_X, LANES), F32)


def smooth_outer(
    lengths_ref, factor_ref, own_ref, plane_ref, rim_ref, rim_plane_ref, box_ref, far_ref, chip_ref,
    inner_ref, shift_ref, given_ref,
    out_ref, placed_ref,
    face_ref, weight_ref, inverse_ref, value_ref, box_rim_ref, edge_ref, sems,
):
    channels = out_ref.shape[0]
    position = lax.axis_index("boxes")
    even_box = position % 2 == 0
    last_box = position == lax.axis_size("boxes") - 1
    work = Smoother(factor_ref, face_ref, weight_ref, inverse_ref, shift_ref, channels, RING)
    lane = work.lane
    sub = lax.broadcasted_iota(jnp.int32, (SUBS, LANES), 0)
    start, box_count = own_run(lengths_ref)

    def send(k):
        rows = pl.ds(pl.multiple_of(k * BOX_X, BOX_X), BOX_X)
        return [
            pltpu.make_async_copy(
                placed_ref.at[j, pl.ds(0, channels), rows],
                out_ref.at[:, rows, pl.ds(j * LANES, LANES)],
                sems.at[k, j],
            )
            for j in range(2)
        ]

    for k in range(1, MOST):
        @pl.when(k >= box_count)
        def _():
            for copy in send(k):
                copy.start()

    def from_after(i):
        return jnp.where(even_box, chip_ref[i], far_ref[i])

    def from_before(i):
        return jnp.where(even_box, far_ref[i], chip_ref[i])

    edges = [
        jnp.where(missing, 0.0, jnp.concatenate([get(40), get(41)], 0))
        for get, missing in ((from_after, last_box), (from_before, position == 0))
    ]
    flat_box = box_ref.reshape(114 * SUBS, LANES)
    conduct = []
    for colour in range(2):
        planes = []
        for j in range(3):
            own = [plane_ref[colour, j, k] if j < 2 else rim_plane_ref[colour, k] for k in range(2)]
            if j < 2:
                row = (((3 * colour + 2) * 8) * 2 + j) * SUBS + 7
                box = flat_box[pl.ds(row, SUBS, stride=2 * SUBS)]
            else:
                box = from_after(38 + colour)
            box = jnp.where(last_box, 0.0, box)
            edge = jnp.zeros((SUBS, LANES), F32)
            for place_at, side, near in ((0, 0, 1), (1, 0, 0), (6, 1, 0), (7, 1, 1)):
                k = colour * 6 + near * 3 + j
                row = jnp.broadcast_to(edges[side][k : k + 1], (SUBS, LANES))
                edge = jnp.where(sub == place_at, row, edge)
            planes.append(jnp.concatenate(own + [box, edge], 0))
        conduct.append(planes)
    work.find_faces(conduct)

    for p in range(8):
        reds, blacks = unpack_halo([from_after(4 * p + i) for i in range(4)], lane)
        for ct in range(3):
            box_rim_ref[0, ct, p], box_rim_ref[1, ct, p] = reds[ct], blacks[ct]
    for ct in range(3):
        for i in range(6):
            edge_ref[0, ct, i] = from_before(ct * 6 + i)
            edge_ref[1, ct, i] = box_ref[96 + ct * 6 + i]
        for colour in range(2):
            edge_ref[0, ct, 6 + colour] = from_before(32 + ct * 2 + colour)
            edge_ref[1, ct, 6 + colour] = from_after(32 + ct * 2 + colour)

    def source_of(q):
        if 2 <= q < 18:
            return lambda colour, ct, j: (
                own_ref[colour, ct, q - 2, j] if j < 2 else rim_ref[colour, ct, q - 2]
            )
        if 18 <= q < 26:
            return lambda colour, ct, j: (
                box_ref[((colour * 3 + ct) * 8 + q - 18) * 2 + j]
                if j < 2
                else box_rim_ref[colour, ct, q - 18]
            )
        near, side = int(q in (1, 26)), int(q > 20)
        return lambda colour, ct, j: edge_ref[side, ct, EDGE.index((colour, near, j))]

    after_exists = jnp.broadcast_to(jnp.logical_not(last_box), (SUBS, LANES))
    before_exists = jnp.broadcast_to(position > 0, (SUBS, LANES))

    def exists(q):
        return before_exists if q < 2 else None if q < 18 else after_exists

    def getter(stage):
        def get(ct, q, j):
            if q - 2 in INNER[stage]:
                return inner_ref[stage, ct, q - 2, j]
            return value_ref[stage, ct, q, j]

        return get

    def putter(stage):
        def put(ct, q, j, value):
            value_ref[stage, ct, q, j] = value

        return put

    def rest(stage, begin, end):
        return [q for q in range(begin, end) if q - 2 not in INNER[stage]]

    zero = jnp.zeros((SUBS, LANES), F32)
    for q in sorted(set(rest(0, 0, 28)) | set(rest(2, 1, 27))):
        wanted = (0, 1) if q in (0, 27) else (0, 1, 2)
        source = source_of(q)
        work.invert(q, 0, source, exists(q), wanted)
        if q - 2 not in INNER[0]:
            for ct in range(3):
                for j in wanted:
                    value_ref[0, ct, q, j] = source(0, ct, j) * inverse_ref[0, ct, q, j]
    for q in (0, 27):
        for ct in range(3):
            value_ref[0, ct, q, 2] = zero
            for j in range(3):
                value_ref[1, ct, q, j] = zero

    for q in sorted(set(rest(1, 1, 27)) | set(rest(3, 2, 26))):
        work.invert(q, 1, source_of(q), exists(q))
    work.update(rest(1, 1, 27), 1, getter(0), putter(1), source_of)
    work.update(rest(2, 1, 27), 0, getter(1), putter(2), source_of)

    place = placer(placed_ref, start, work.even)
    for begin, end, boxes in ((2, 18, (0, 1)), (18, 26, (2,))):
        places = rest(3, begin, end)
        work.update(places, 1, getter(2), putter(3), source_of, (0, 1))
        for box in boxes:
            @pl.when((box >= start) & (box < start + box_count))
            def _():
                for q in places:
                    if (q - 2) // 8 == box:
                        for ct in range(3):
                            for j in range(2):
                                place(ct, q, j, getter(2)(ct, q, j), value_ref[3, ct, q, j])
                for copy in send(box - start):
                    copy.start()

    for k in range(MOST):
        for copy in send(k):
            copy.wait()


def in_vmem(count):
    return [pl.BlockSpec(memory_space=pltpu.VMEM)] * count


def on_device(sources, absorption, conductance, diffusivity, run_lengths):
    channels, planes, cells = sources.shape
    boxes, groups = lax.axis_size("boxes"), lax.axis_size("grp")
    pairs = planes // 2
    real = lambda *shape: jax.ShapeDtypeStruct(shape + (SUBS, LANES), F32)
    vmem = lambda *shape: pltpu.VMEM(shape + (SUBS, LANES), F32)
    params = pltpu.CompilerParams(vmem_limit_bytes=VMEM_LIMIT)
    own, plane, first, second, box = pl.pallas_call(
        pack_rims,
        out_shape=(
            real(2, 3, pairs, 2),
            real(2, 2, 2),
            real(2 * pairs + 2),
            real(2 * pairs + 2),
            real(114),
        ),
        in_specs=in_vmem(1),
        out_specs=tuple(in_vmem(5)),
        scratch_shapes=[pltpu.VMEM((2, channels + 2, planes, LANES), F32)],
        compiler_params=params,
    )(jnp.concatenate([sources, absorption[None], conductance[None]]))
    second = lax.ppermute(second, ("boxes", "grp"), swap_pairs(boxes, groups, False, 1))
    first = lax.ppermute(first, ("boxes", "grp"), swap_pairs(boxes, groups, False, 0))
    box = lax.ppermute(box, "boxes", [((i + 1) % boxes, i) for i in range(boxes)])
    rim, rim_plane, chip, far = pl.pallas_call(
        pack_faces,
        out_shape=(real(2, 3, pairs), real(2, 2), real(42), real(42)),
        in_specs=in_vmem(4),
        out_specs=tuple(in_vmem(4)),
        compiler_params=params,
    )(own, plane, first, second)
    chip = lax.ppermute(chip, ("boxes", "grp"), swap_pairs(boxes, groups, True, 0))
    far = lax.ppermute(far, ("boxes", "grp"), swap_pairs(boxes, groups, True, 1))
    smem = pl.BlockSpec(memory_space=pltpu.SMEM)
    placed_shape = (2, 3 * SUBS, MOST * BOX_X, LANES)
    inner, placed, shift = pl.pallas_call(
        smooth_inner,
        out_shape=(
            real(4, 3, pairs, 3),
            jax.ShapeDtypeStruct(placed_shape, F32),
            jax.ShapeDtypeStruct((2, 2 * LANES, 2 * LANES), jnp.bfloat16),
        ),
        in_specs=[smem, smem] + in_vmem(4),
        out_specs=tuple(in_vmem(3)),
        scratch_shapes=[
            pltpu.VMEM((2, 6, 3, pairs, LANES), F32),
            pltpu.VMEM((2, 3, pairs, LANES), F32),
            vmem(2, 3, pairs + 2, 3),
        ],
        compiler_params=params,
        cost_estimate=pl.CostEstimate(flops=2_000_000_000, bytes_accessed=0, transcendentals=0),
    )(run_lengths, diffusivity, own, plane, rim, rim_plane)
    correction, _ = pl.pallas_call(
        smooth_outer,
        out_shape=(
            jax.ShapeDtypeStruct((channels, MOST * BOX_X, cells), F32),
            jax.ShapeDtypeStruct(placed_shape, F32),
        ),
        in_specs=[smem, smem] + in_vmem(10),
        out_specs=(pl.BlockSpec(memory_space=pltpu.HBM), in_vmem(1)[0]),
        input_output_aliases={11: 1},
        scratch_shapes=[
            pltpu.VMEM((2, 6, 3, RING, LANES), F32),
            pltpu.VMEM((2, 3, RING, LANES), F32),
            vmem(2, 3, 28, 3),
            vmem(4, 3, 28, 3),
            vmem(2, 3, 8),
            vmem(2, 3, 8),
            pltpu.SemaphoreType.DMA((MOST, 2)),
        ],
        compiler_params=params,
    )(run_lengths, diffusivity, own, plane, rim, rim_plane, box, far, chip, inner, shift, placed)
    return correction


def solution(mesh):
    return jax.shard_map(
        on_device,
        mesh=mesh,
        in_specs=(P(None, "boxes", "grp"), P("boxes", "grp"), P("boxes", "grp"), P(), P()),
        out_specs=P(None, "boxes", "grp"),
        check_vma=False,
    )
```

```python
import jax
import jax.numpy as jnp
from jax import lax
from jax.experimental import pallas as pl
from jax.experimental.pallas import tpu as pltpu
from jax.sharding import PartitionSpec as P

BOX_X = 16
PLANE_Z = 16
OLD_DEV = 2
MOST = 3
LANES = 128
SUBS = 8
RING = 32
RIM = 64
VMEM_LIMIT = 40 * 1024 * 1024
F32 = jnp.float32


def swap_pairs(boxes, groups, along_boxes, first):
    count, other = (boxes, groups) if along_boxes else (groups, boxes)
    pairs = []
    for i in range(count):
        k = i + 1 if (i - first) % 2 == 0 else i - 1
        for m in range(other):
            here, there = (i, m), (k, m)
            if not 0 <= k < count:
                there = (i, m ^ 1)
                if (m ^ 1) >= other:
                    continue
            if not along_boxes:
                here, there = here[::-1], there[::-1]
            pairs.append(tuple(b * groups + g for b, g in (here, there)))
    return pairs


def lane_places(rows):
    lane = lax.broadcasted_iota(jnp.int32, (rows, LANES), 1)
    even = (lane + lane // PLANE_Z) % 2 == 0
    return lane, even


def roll(x, shift):
    return pltpu.roll(x, shift % LANES, 1) if shift % LANES else x


def pack_rim(red, black, lane, high):
    red_from, black_from = (LANES - 48, LANES - 32) if high else (0, 0)
    reds = [roll(x, to - red_from) for x, to in zip(red, (0, 64, 64))]
    first = jnp.where(lane < 64, reds[0], reds[1])
    first = jnp.where((lane >= 48) & (lane < 64), roll(black[2], 48 - black_from), first)
    first = jnp.where(lane >= 112, roll(black[2], 96 - black_from), first)
    second = jnp.where(lane < 64, roll(black[1], 32 - black_from), reds[2])
    second = jnp.where(lane < 32, roll(black[0], -black_from), second)
    return first, second


def unpack_rim(first, second, lane, high):
    red_to, black_to = (LANES - 48, LANES - 32) if high else (0, 0)
    red = [roll(first, red_to), roll(first, red_to - 64), roll(second, red_to - 64)]
    black = [roll(second, black_to), roll(second, black_to - 32)]
    black.append(jnp.where(lane < black_to + 16, roll(first, black_to - 48), roll(first, black_to - 96)))
    return red, black


def pack_halo(red, black, lane):
    gap = (lane >= 48) & (lane < 80)
    wide = (lane >= 32) & (lane < 96)
    return [
        jnp.where(gap, roll(black[2], 48), red[0]),
        jnp.where(gap, roll(black[2], -48), red[1]),
        red[2],
        jnp.where(wide, roll(black[1], 64), black[0]),
    ]


def unpack_halo(parts, lane):
    black = jnp.where(lane < 64, roll(parts[0], -48), roll(parts[1], 48))
    return parts[:3], [parts[3], roll(parts[3], 64), black]


def pack_rims(
    src_ref,
    own_ref, plane_ref, first_ref, second_ref, third_ref, box_ref,
    tiles_ref,
):
    layers, planes, _ = src_ref.shape
    channels = layers - 2
    half = planes // 2
    for layer in range(layers):
        for j in range(2):
            lanes = pl.ds(j * LANES, LANES)
            tiles_ref[j, layer] = src_ref[layer, :, lanes]

    lane, even = lane_places(SUBS)
    even_group = lax.axis_index("grp") % 2 == 0
    flat = tiles_ref.reshape(2 * layers * planes, LANES)

    for p in range(half):
        reds, blacks = [], []
        for j in range(2):
            red, black = [], []
            for ct in range(3):
                row = (j * layers + ct * SUBS) * planes + 2 * p
                low = flat[pl.ds(row, SUBS, stride=planes)]
                high = flat[pl.ds(row + 1, SUBS, stride=planes)]
                red.append(jnp.where(even, low, high))
                black.append(jnp.where(even, high, low))
                own_ref[0, ct, p, j] = red[ct]
                own_ref[1, ct, p, j] = black[ct]
                if p < 8:
                    box_ref[(ct * 8 + p) * 2 + j] = red[ct]
                    box_ref[((3 + ct) * 8 + p) * 2 + j] = black[ct]
                if p in (8, 9):
                    near = int(p == 8)
                    box_ref[96 + ct * 6 + EDGE.index((0, near, j))] = red[ct]
                    if near:
                        box_ref[96 + ct * 6 + EDGE.index((1, near, j))] = black[ct]
            reds.append(red)
            blacks.append(black)
        low_rim = pack_rim(reds[0], blacks[0], lane, False)
        high_rim = pack_rim(reds[1], blacks[1], lane, True)
        for i in range(2):
            first_ref[2 * p + i] = jnp.where(even_group, high_rim[i], low_rim[i])
            third_ref[2 * p + i] = jnp.where(even_group, high_rim[i], low_rim[i])
            second_ref[2 * p + i] = jnp.where(even_group, low_rim[i], high_rim[i])

    for q in range(2):
        compact = []
        for j in range(2):
            row = (j * layers + channels + 1) * planes + 16 * q
            low = flat[pl.ds(row, SUBS, stride=2)]
            high = flat[pl.ds(row + 1, SUBS, stride=2)]
            compact.append((jnp.where(even, low, high), jnp.where(even, high, low)))
            for colour in range(2):
                plane_ref[colour, j, q] = compact[j][colour]
        low_rim = jnp.where(lane < RIM, compact[0][0], roll(compact[0][1], RIM))
        high_rim = jnp.where(lane < RIM, roll(compact[1][0], RIM), compact[1][1])
        first_ref[2 * half + q] = jnp.where(even_group, high_rim, low_rim)
        third_ref[2 * half + q] = jnp.where(even_group, high_rim, low_rim)
        second_ref[2 * half + q] = jnp.where(even_group, low_rim, high_rim)


def pack_faces(own_ref, plane_ref, first_ref, second_ref, third_ref, rim_ref, rim_plane_ref, down_ref, up_ref):
    pairs = own_ref.shape[2]
    lane, _ = lane_places(SUBS)
    low_half = lane < RIM
    group = lax.axis_index("grp")
    even_group = group % 2 == 0
    early = group // 2 % 2 == 0

    def sides(i):
        first, second = jnp.where(early, first_ref[i], third_ref[i]), second_ref[i]
        return jnp.where(even_group, first, second), jnp.where(even_group, second, first)

    for p in range(pairs):
        above, below = zip(*[sides(2 * p + i) for i in range(2)])
        above, below = unpack_rim(*above, lane, False), unpack_rim(*below, lane, True)
        reds, blacks = [], []
        for ct in range(3):
            reds.append(jnp.where(low_half, above[0][ct], below[0][ct]))
            blacks.append(jnp.where(low_half, above[1][ct], below[1][ct]))
            rim_ref[0, ct, p] = reds[ct]
            rim_ref[1, ct, p] = blacks[ct]
        if p < 8:
            for i, part in enumerate(pack_halo(reds, blacks, lane)):
                down_ref[4 * p + i] = part
    for q in range(2):
        above, below = sides(2 * pairs + q)
        above = jnp.where(group == lax.axis_size("grp") - 1, 0.0, above)
        below = jnp.where(group == 0, 0.0, below)
        rim_plane_ref[0, q] = jnp.where(low_half, above, roll(below, RIM))
        rim_plane_ref[1, q] = jnp.where(low_half, roll(above, RIM), below)

    for colour in range(2):
        for ct in range(3):
            down_ref[32 + ct * 2 + colour] = rim_ref[colour, ct, 8]
            up_ref[18 + ct * 2 + colour] = rim_ref[colour, ct, 15]
        down_ref[38 + colour] = rim_plane_ref[colour, 0]
    for ct in range(3):
        for i, (colour, near, j) in enumerate(EDGE[:6]):
            up_ref[ct * 6 + i] = own_ref[colour, ct, 15 if near else 14, j]
    for colour in range(2):
        for near in range(2):
            for j in range(3):
                down, up = (0, 7) if near else (1, 6)
                rows = [
                    (plane_ref[colour, j, 1] if j < 2 else rim_plane_ref[colour, 1])[k : k + 1]
                    for k in (down, up)
                ]
                k = colour * 6 + near * 3 + j
                down_ref[40 + k // 8, k % 8 : k % 8 + 1] = rows[0]
                up_ref[24 + k // 8, k % 8 : k % 8 + 1] = rows[1]
    down_ref[41, 4:8] = jnp.zeros((4, LANES), F32)
    up_ref[25, 4:8] = jnp.zeros((4, LANES), F32)


EDGE = [(0, 1, 0), (0, 1, 1), (0, 0, 0), (0, 0, 1), (1, 1, 0), (1, 1, 1), (0, 1, 2), (1, 1, 2)]


def shift_matrices():
    row = lax.broadcasted_iota(jnp.int32, (2 * LANES, LANES), 0) % LANES
    col = lax.broadcasted_iota(jnp.int32, (2 * LANES, LANES), 1)
    z = col % PLANE_Z
    pick = lambda source: jnp.where(row == source, 1.0, 0.0)
    along_z = [pick(col - z + (z + step) % PLANE_Z) for step in (1, PLANE_Z - 1)]
    along_y = [pick((col + step) % LANES) for step in (PLANE_Z, LANES - PLANE_Z)]
    return [jnp.concatenate(pair, 1).astype(jnp.bfloat16) for pair in (along_z, along_y)]


def z_up(x, z):
    return jnp.where(z == PLANE_Z - 1, roll(x, PLANE_Z - 1), roll(x, -1))


def z_down(x, z):
    return jnp.where(z == 0, roll(x, 1 - PLANE_Z), roll(x, 1))


def lane_neighbours(tiles, lane, wanted=(0, 1, 2)):
    z = lane % PLANE_Z
    up = [roll(x, -PLANE_Z) for x in tiles]
    down = [roll(x, PLANE_Z) for x in tiles]
    return [
        [
            z_up(tiles[j], z),
            z_down(tiles[j], z),
            jnp.where(lane < LANES - PLANE_Z, up[j], up[(j + 1) % 3]),
            jnp.where(lane < PLANE_Z, down[(j + 2) % 3], down[j]),
        ]
        for j in wanted
    ]


INNER = [range(1, 15), range(1, 15), range(2, 14), range(2, 14)]


class Smoother:
    def __init__(self, factor_ref, face_ref, weight_ref, inverse_ref, shift_ref, channels, ring):
        self.face_ref, self.weight_ref, self.inverse_ref = face_ref, weight_ref, inverse_ref
        self.shift_ref, self.ring = shift_ref, ring
        self.lane, self.even = lane_places(SUBS)
        sub = lax.broadcasted_iota(jnp.int32, (SUBS, LANES), 0)
        group = lax.axis_index("grp")
        above = jnp.where(group == lax.axis_size("grp") - 1, 0, LANES)
        below = jnp.where(group == 0, LANES, 0)
        self.limit = [
            ((self.lane < jnp.minimum(above, PLANE_Z * rows)))
            | (self.lane >= jnp.maximum(below, LANES - PLANE_Z * rows))
            for rows in (3, 2)
        ]
        self.factors = []
        for ct in range(3):
            factor = jnp.zeros((SUBS, LANES), F32)
            for i in range(min(SUBS, channels - ct * SUBS)):
                factor = jnp.where(sub == i, 0.5 * factor_ref[ct * SUBS + i], factor)
            self.factors.append(factor)

    def find_faces(self, conduct):
        wide_lane, wide_even = lane_places(self.ring)
        for colour in range(2):
            others = conduct[1 - colour]
            beside = lane_neighbours(others, wide_lane)
            for j in range(3):
                after, before = pltpu.roll(others[j], self.ring - 1, 0), pltpu.roll(others[j], 1, 0)
                across = jnp.where(wide_even, *((before, after) if colour == 0 else (after, before)))
                total = jnp.zeros((self.ring, LANES), F32)
                for i, other in enumerate([others[j], across] + beside[j]):
                    face = conduct[colour][j] + other
                    self.face_ref[colour, i, j] = face
                    total = total + face
                self.weight_ref[colour, j] = total

    def spread(self, ref, index, q):
        row = (q + RING - 2) % RING
        return jnp.broadcast_to(ref[index + (pl.ds(row, 1),)], (SUBS, LANES))

    def invert(self, q, colour, source, exists, wanted=(0, 1, 2)):
        for j in wanted:
            absorb = jnp.broadcast_to(source(colour, 2, j)[6:7], (SUBS, LANES))
            weight = self.spread(self.weight_ref, (colour, j), q)
            keep = exists if j < 2 else self.limit[colour]
            if exists is not None and j == 2:
                keep = keep & exists
            for ct in range(3):
                inverse = 1.0 / (absorb + self.factors[ct] * weight)
                if keep is not None:
                    inverse = jnp.where(keep, inverse, 0.0)
                self.inverse_ref[colour, ct, q, j] = inverse

    def shifted(self, places, get):
        index = [(ct, q, j) for q in places for ct in range(3) for j in range(3)]
        x = jnp.concatenate([get(*key) for key in index], 0)
        high = x.astype(jnp.bfloat16)
        both = jnp.concatenate([high, (x - high.astype(F32)).astype(jnp.bfloat16)], 1)
        moved = [jnp.dot(both, self.shift_ref[i], preferred_element_type=F32) for i in range(2)]
        result = {}
        for k, key in enumerate(index):
            rows = slice(k * SUBS, (k + 1) * SUBS)
            result[key] = [m[rows, i * LANES : (i + 1) * LANES] for m in moved for i in range(2)]
        return result

    def update(self, places, colour, get, put, source_of, wanted=(0, 1, 2)):
        lane, even = self.lane, self.even
        moved = self.shifted(places, get)
        for q in places:
            source = source_of(q)
            faces = [
                [self.spread(self.face_ref, (colour, i, j), q) for i in range(6)] for j in wanted
            ]
            for ct in range(3):
                near = [moved[ct, q, j] for j in range(3)]
                for j, face in zip(wanted, faces):
                    before, after = get(ct, q - 1, j), get(ct, q + 1, j)
                    across = jnp.where(even, *((before, after) if colour == 0 else (after, before)))
                    up = jnp.where(lane < LANES - PLANE_Z, near[j][2], near[(j + 1) % 3][2])
                    down = jnp.where(lane < PLANE_Z, near[(j + 2) % 3][3], near[j][3])
                    inflow = face[0] * get(ct, q, j)
                    for one, other in zip(face[1:], [across, near[j][0], near[j][1], up, down]):
                        inflow = inflow + one * other
                    value = source(colour, ct, j) + self.factors[ct] * inflow
                    put(ct, q, j, value * self.inverse_ref[colour, ct, q, j])


def own_run(lengths_ref):
    position = lax.axis_index("boxes")
    first_box = lax.fori_loop(0, position, lambda i, total: total + lengths_ref[i], jnp.int32(0))
    return first_box - position * OLD_DEV, lengths_ref[position]


def placer(placed_ref, start, even):
    rows = placed_ref.shape[2]
    flat = placed_ref.reshape(2 * 3 * SUBS * rows, LANES)

    def place(ct, q, j, red, black):
        row = (j * 3 + ct) * SUBS * rows + 2 * (q - 2 - 8 * start)
        flat[pl.ds(row, SUBS, stride=rows)] = jnp.where(even, red, black)
        flat[pl.ds(row + 1, SUBS, stride=rows)] = jnp.where(even, black, red)

    return place


def smooth_inner(
    lengths_ref, factor_ref, own_ref, plane_ref, rim_ref, rim_plane_ref,
    value_ref, placed_ref, shift_ref,
    face_ref, weight_ref, inverse_ref,
):
    pairs = own_ref.shape[2]
    channels = factor_ref.shape[0]
    work = Smoother(factor_ref, face_ref, weight_ref, inverse_ref, shift_ref, channels, pairs)
    for i, matrix in enumerate(shift_matrices()):
        shift_ref[i] = matrix

    def plane(colour, j):
        return [plane_ref[colour, j, k] if j < 2 else rim_plane_ref[colour, k] for k in range(2)]

    work.find_faces(
        [[jnp.concatenate(plane(colour, j), 0) for j in range(3)] for colour in range(2)]
    )

    def source_of(q):
        p = q - 2
        return lambda colour, ct, j: own_ref[colour, ct, p, j] if j < 2 else rim_ref[colour, ct, p]

    def getter(stage):
        return lambda ct, q, j: value_ref[stage, ct, q - 2, j]

    def putter(stage):
        def put(ct, q, j, value):
            value_ref[stage, ct, q - 2, j] = value

        return put

    for p in range(pairs):
        source = source_of(p + 2)
        work.invert(p + 2, 0, source, None)
        work.invert(p + 2, 1, source, None)
        for ct in range(3):
            for j in range(3):
                value_ref[0, ct, p, j] = source(0, ct, j) * inverse_ref[0, ct, p + 2, j]
    for p in (0, pairs - 1):
        for ct in range(3):
            for j in range(3):
                value_ref[1, ct, p, j] = jnp.zeros((SUBS, LANES), F32)
    for places in (range(3, 11), range(11, 17)):
        work.update(places, 1, getter(0), putter(1), source_of)
    for places in (range(3, 11), range(11, 17)):
        work.update(places, 0, getter(1), putter(2), source_of)
    for places in (range(4, 10), range(10, 16)):
        work.update(places, 1, getter(2), putter(3), source_of, (0, 1))

    start, box_count = own_run(lengths_ref)
    place = placer(placed_ref, start, work.even)
    for box, places in enumerate((range(4, 10), range(10, 16))):
        @pl.when((box >= start) & (box < start + box_count))
        def _():
            for q in places:
                for ct in range(3):
                    for j in range(2):
                        place(ct, q, j, getter(2)(ct, q, j), getter(3)(ct, q, j))

    for k in range(1, MOST):
        @pl.when(k >= box_count)
        def _():
            for j in range(2):
                for c in range(channels):
                    placed_ref[j, c, k * BOX_X : (k + 1) * BOX_X] = jnp.zeros((BOX_X, LANES), F32)


def smooth_outer(
    lengths_ref, factor_ref, own_ref, plane_ref, rim_ref, rim_plane_ref, box_ref, down_ref, up_ref,
    inner_ref, shift_ref, given_ref,
    out_ref, placed_ref,
    face_ref, weight_ref, inverse_ref, value_ref, box_rim_ref, edge_ref, sems,
):
    channels = out_ref.shape[0]
    position = lax.axis_index("boxes")
    last_box = position == lax.axis_size("boxes") - 1
    work = Smoother(factor_ref, face_ref, weight_ref, inverse_ref, shift_ref, channels, RING)
    lane = work.lane
    sub = lax.broadcasted_iota(jnp.int32, (SUBS, LANES), 0)
    start, box_count = own_run(lengths_ref)

    def send(k):
        rows = pl.ds(pl.multiple_of(k * BOX_X, BOX_X), BOX_X)
        return [
            pltpu.make_async_copy(
                placed_ref.at[j, pl.ds(0, channels), rows],
                out_ref.at[:, rows, pl.ds(j * LANES, LANES)],
                sems.at[k, j],
            )
            for j in range(2)
        ]

    for k in range(1, MOST):
        @pl.when(k >= box_count)
        def _():
            for copy in send(k):
                copy.start()

    edges = [
        jnp.where(missing, 0.0, jnp.concatenate([ref[i], ref[i + 1]], 0))
        for ref, i, missing in ((down_ref, 40, last_box), (up_ref, 24, position == 0))
    ]
    flat_box = box_ref.reshape(114 * SUBS, LANES)
    conduct = []
    for colour in range(2):
        planes = []
        for j in range(3):
            own = [plane_ref[colour, j, k] if j < 2 else rim_plane_ref[colour, k] for k in range(2)]
            if j < 2:
                row = (((3 * colour + 2) * 8) * 2 + j) * SUBS + 7
                box = flat_box[pl.ds(row, SUBS, stride=2 * SUBS)]
            else:
                box = down_ref[38 + colour]
            box = jnp.where(last_box, 0.0, box)
            edge = jnp.zeros((SUBS, LANES), F32)
            for place_at, side, near in ((0, 0, 1), (1, 0, 0), (6, 1, 0), (7, 1, 1)):
                k = colour * 6 + near * 3 + j
                row = jnp.broadcast_to(edges[side][k : k + 1], (SUBS, LANES))
                edge = jnp.where(sub == place_at, row, edge)
            planes.append(jnp.concatenate(own + [box, edge], 0))
        conduct.append(planes)
    work.find_faces(conduct)

    for p in range(8):
        reds, blacks = unpack_halo([down_ref[4 * p + i] for i in range(4)], lane)
        for ct in range(3):
            box_rim_ref[0, ct, p], box_rim_ref[1, ct, p] = reds[ct], blacks[ct]
    for ct in range(3):
        for i in range(6):
            edge_ref[0, ct, i] = up_ref[ct * 6 + i]
            edge_ref[1, ct, i] = box_ref[96 + ct * 6 + i]
        for colour in range(2):
            edge_ref[0, ct, 6 + colour] = up_ref[18 + ct * 2 + colour]
            edge_ref[1, ct, 6 + colour] = down_ref[32 + ct * 2 + colour]

    def source_of(q):
        if 2 <= q < 18:
            return lambda colour, ct, j: (
                own_ref[colour, ct, q - 2, j] if j < 2 else rim_ref[colour, ct, q - 2]
            )
        if 18 <= q < 26:
            return lambda colour, ct, j: (
                box_ref[((colour * 3 + ct) * 8 + q - 18) * 2 + j]
                if j < 2
                else box_rim_ref[colour, ct, q - 18]
            )
        near, side = int(q in (1, 26)), int(q > 20)
        return lambda colour, ct, j: edge_ref[side, ct, EDGE.index((colour, near, j))]

    after_exists = jnp.broadcast_to(jnp.logical_not(last_box), (SUBS, LANES))
    before_exists = jnp.broadcast_to(position > 0, (SUBS, LANES))

    def exists(q):
        return before_exists if q < 2 else None if q < 18 else after_exists

    def getter(stage):
        def get(ct, q, j):
            if q - 2 in INNER[stage]:
                return inner_ref[stage, ct, q - 2, j]
            return value_ref[stage, ct, q, j]

        return get

    def putter(stage):
        def put(ct, q, j, value):
            value_ref[stage, ct, q, j] = value

        return put

    def rest(stage, begin, end):
        return [q for q in range(begin, end) if q - 2 not in INNER[stage]]

    zero = jnp.zeros((SUBS, LANES), F32)
    for q in sorted(set(rest(0, 0, 28)) | set(rest(2, 1, 27))):
        wanted = (0, 1) if q in (0, 27) else (0, 1, 2)
        source = source_of(q)
        work.invert(q, 0, source, exists(q), wanted)
        if q - 2 not in INNER[0]:
            for ct in range(3):
                for j in wanted:
                    value_ref[0, ct, q, j] = source(0, ct, j) * inverse_ref[0, ct, q, j]
    for q in (0, 27):
        for ct in range(3):
            value_ref[0, ct, q, 2] = zero
            for j in range(3):
                value_ref[1, ct, q, j] = zero

    for q in sorted(set(rest(1, 1, 27)) | set(rest(3, 2, 26))):
        work.invert(q, 1, source_of(q), exists(q))
    work.update(rest(1, 1, 27), 1, getter(0), putter(1), source_of)
    work.update(rest(2, 1, 27), 0, getter(1), putter(2), source_of)

    place = placer(placed_ref, start, work.even)
    for begin, end, boxes in ((2, 18, (0, 1)), (18, 26, (2,))):
        places = rest(3, begin, end)
        work.update(places, 1, getter(2), putter(3), source_of, (0, 1))
        for box in boxes:
            @pl.when((box >= start) & (box < start + box_count))
            def _():
                for q in places:
                    if (q - 2) // 8 == box:
                        for ct in range(3):
                            for j in range(2):
                                place(ct, q, j, getter(2)(ct, q, j), value_ref[3, ct, q, j])
                for copy in send(box - start):
                    copy.start()

    for k in range(MOST):
        for copy in send(k):
            copy.wait()


def in_vmem(count):
    return [pl.BlockSpec(memory_space=pltpu.VMEM)] * count


def on_device(sources, absorption, conductance, diffusivity, run_lengths):
    channels, planes, cells = sources.shape
    boxes, groups = lax.axis_size("boxes"), lax.axis_size("grp")
    pairs = planes // 2
    real = lambda *shape: jax.ShapeDtypeStruct(shape + (SUBS, LANES), F32)
    vmem = lambda *shape: pltpu.VMEM(shape + (SUBS, LANES), F32)
    params = pltpu.CompilerParams(vmem_limit_bytes=VMEM_LIMIT)
    own, plane, first, second, third, box = pl.pallas_call(
        pack_rims,
        out_shape=(
            real(2, 3, pairs, 2),
            real(2, 2, 2),
            real(2 * pairs + 2),
            real(2 * pairs + 2),
            real(2 * pairs + 2),
            real(114),
        ),
        in_specs=in_vmem(1),
        out_specs=tuple(in_vmem(6)),
        scratch_shapes=[pltpu.VMEM((2, channels + 2, planes, LANES), F32)],
        compiler_params=params,
    )(jnp.concatenate([sources, absorption[None], conductance[None]]))
    near = swap_pairs(boxes, groups, False, 0)
    beside = [(i, (i // groups ^ 1) * groups + i % groups) for i in range(boxes * groups)]

    def turn(which):
        return [
            pair if pair[0] % groups // 2 % 2 == which else beside[pair[0]] for pair in near
        ]

    third = lax.ppermute(third, ("boxes", "grp"), turn(1))
    second = lax.ppermute(second, ("boxes", "grp"), swap_pairs(boxes, groups, False, 1))
    first = lax.ppermute(first, ("boxes", "grp"), turn(0))
    box = lax.ppermute(box, "boxes", [((i + 1) % boxes, i) for i in range(boxes)])
    rim, rim_plane, down, up = pl.pallas_call(
        pack_faces,
        out_shape=(real(2, 3, pairs), real(2, 2), real(42), real(26)),
        in_specs=in_vmem(5),
        out_specs=tuple(in_vmem(4)),
        compiler_params=params,
    )(own, plane, first, second, third)
    down = lax.ppermute(down, "boxes", [((i + 1) % boxes, i) for i in range(boxes)])
    up = lax.ppermute(up, "boxes", [(i, (i + 1) % boxes) for i in range(boxes)])
    smem = pl.BlockSpec(memory_space=pltpu.SMEM)
    placed_shape = (2, 3 * SUBS, MOST * BOX_X, LANES)
    inner, placed, shift = pl.pallas_call(
        smooth_inner,
        out_shape=(
            real(4, 3, pairs, 3),
            jax.ShapeDtypeStruct(placed_shape, F32),
            jax.ShapeDtypeStruct((2, 2 * LANES, 2 * LANES), jnp.bfloat16),
        ),
        in_specs=[smem, smem] + in_vmem(4),
        out_specs=tuple(in_vmem(3)),
        scratch_shapes=[
            pltpu.VMEM((2, 6, 3, pairs, LANES), F32),
            pltpu.VMEM((2, 3, pairs, LANES), F32),
            vmem(2, 3, pairs + 2, 3),
        ],
        compiler_params=params,
        cost_estimate=pl.CostEstimate(flops=4_000_000_000, bytes_accessed=0, transcendentals=0),
    )(run_lengths, diffusivity, own, plane, rim, rim_plane)
    correction, _ = pl.pallas_call(
        smooth_outer,
        out_shape=(
            jax.ShapeDtypeStruct((channels, MOST * BOX_X, cells), F32),
            jax.ShapeDtypeStruct(placed_shape, F32),
        ),
        in_specs=[smem, smem] + in_vmem(10),
        out_specs=(pl.BlockSpec(memory_space=pltpu.HBM), in_vmem(1)[0]),
        input_output_aliases={11: 1},
        scratch_shapes=[
            pltpu.VMEM((2, 6, 3, RING, LANES), F32),
            pltpu.VMEM((2, 3, RING, LANES), F32),
            vmem(2, 3, 28, 3),
            vmem(4, 3, 28, 3),
            vmem(2, 3, 8),
            vmem(2, 3, 8),
            pltpu.SemaphoreType.DMA((MOST, 2)),
        ],
        compiler_params=params,
    )(run_lengths, diffusivity, own, plane, rim, rim_plane, box, down, up, inner, shift, placed)
    return correction


def solution(mesh):
    return jax.shard_map(
        on_device,
        mesh=mesh,
        in_specs=(P(None, "boxes", "grp"), P("boxes", "grp"), P("boxes", "grp"), P(), P()),
        out_specs=P(None, "boxes", "grp"),
        check_vma=False,
    )
```
